512 devices in a mesh: branch: 4 (over z_hi), row: 16 (over y, core), col: 8 (over z_lo, x).
Axes of the slice: x: 4, y: 8, z: 8 (z_hi: 4, z_lo: 2; z = z_hi * 2 + z_lo), core: 2. Of those that a mesh axis runs over, the one named last changes fastest.
Arguments:
- homolog_tensor: bfloat16 [256, 128, 256], P('col', 'row'), may hold values from -6 to 6
- couple_tensor: bfloat16 [128, 128, 128], P('row', 'col'), may hold values from -6 to 6
- probe_matrix: bfloat16 [256, 256], P(None, 'branch'), may hold values from -0.375 to 0.375
- lookup_matrix: bfloat16 [256, 256], P(None, 'branch'), may hold values from -0.375 to 0.375
- content_matrix: bfloat16 [256, 256], P(None, 'branch'), may hold values from -0.375 to 0.375
- scoring_sigmoid_matrix: bfloat16 [256, 256], P(None, 'branch'), may hold values from -0.375 to 0.375
- scoring_final_matrix: bfloat16 [256, 256], P('branch'), may hold values from -0.375 to 0.375
- couple_offset_matrix: bfloat16 [128, 8], P(None, 'branch'), may hold values from -43 to 43
- product_first_matrix: bfloat16 [256, 32], replicated, may hold values from -0.375 to 0.375
- product_second_matrix: bfloat16 [256, 32], replicated, may hold values from -0.375 to 0.375
- product_final_matrix: bfloat16 [1024, 128], replicated, may hold values from -1 to 1
- trio_first_matrix: bfloat16 [2, 128, 128], P(None, None, 'branch'), may hold values from -0.5 to 0.5
- trio_second_matrix: bfloat16 [2, 128, 128], P(None, None, 'branch'), may hold values from -0.5 to 0.5
- trio_sigmoid_matrix: bfloat16 [128, 128], replicated, may hold values from -0.5 to 0.5
- trio_final_matrix: bfloat16 [128, 128], replicated, may hold values from -0.5 to 0.5
Outputs:
- revised_homolog_matrix: bfloat16 [256, 128, 256], P('col', 'row', 'branch')
- pairwise_output: bfloat16 [128, 128, 128], P('row', 'col')
The draws below stay inside these ranges and needn't reach their ends.
All inputs are finite; a program needn't handle non-finite values.
Results may differ from the reference program's by a relative error of at most 0.014.
Values may be sent and summed in bfloat16 or wider, within the bound.
A program may use at most 64 MiB of HBM per device.

```python
import jax
import jax.numpy as jnp
from jax import lax

ROW_CHANNELS = 256
CP = 128
NUM_SUBSPACES = 8
SUBSPACE_SIZE = 32
PROJ_CHANNELS = 32
NUM_POSITIONS = 128
NUM_HOMOLOGS = 256


def draw_couple_offset_matrix(key, part):
    first, second = jax.random.split(jax.random.fold_in(key, 7))
    base = jnp.clip(jax.random.normal(first, (CP, NUM_SUBSPACES), jnp.float32), -4.0, 4.0) * 0.088
    scales = jax.random.uniform(second, (1, NUM_SUBSPACES), jnp.float32, 0.5, 2.0)
    return (base * scales).astype(jnp.bfloat16)


def block_scale(own_key, shape, shards, least, largest):
    def one(dim, shards_of):
        heights = jax.random.uniform(jax.random.fold_in(jax.random.fold_in(own_key, 6), dim), (shards_of,), jnp.float32, least / len(shards), largest / len(shards))
        return jnp.repeat(jnp.exp(heights), shape[dim] // shards_of).reshape((-1,) + (1,) * (len(shape) - dim - 1))

    gain = one(*shards[0])
    for cut in shards[1:]:
        gain = gain * one(*cut)
    return gain


def scatter_about(stream_key, shape, deviation, reach, shards=(), dtype=jnp.bfloat16):
    result = deviation * jax.random.normal(stream_key, shape, jnp.float32)
    if shards:
        result = result * block_scale(stream_key, shape, shards, -0.22, 0.18)
    return jnp.clip(result, -reach, reach).astype(dtype)


def setup_inputs(seed: int = 0) -> dict:
    splits = jax.random.split(jax.random.key(seed), 16)
    return {
        "homolog_tensor": scatter_about(splits[0], (NUM_HOMOLOGS, NUM_POSITIONS, ROW_CHANNELS), 1.0, 6.0, ((0, 8), (1, 16))),
        "couple_tensor": scatter_about(splits[1], (NUM_POSITIONS, NUM_POSITIONS, CP), 1.0, 6.0, ((0, 16), (1, 8))),
        "probe_matrix": scatter_about(splits[2], (ROW_CHANNELS, NUM_SUBSPACES * SUBSPACE_SIZE), ROW_CHANNELS ** -0.5, 0.375, ((1, 4),)),
        "lookup_matrix": scatter_about(splits[3], (ROW_CHANNELS, NUM_SUBSPACES * SUBSPACE_SIZE), ROW_CHANNELS ** -0.5, 0.375, ((1, 4),)),
        "content_matrix": scatter_about(splits[4], (ROW_CHANNELS, NUM_SUBSPACES * SUBSPACE_SIZE), ROW_CHANNELS ** -0.5, 0.375, ((1, 4),)),
        "scoring_sigmoid_matrix": scatter_about(splits[5], (ROW_CHANNELS, NUM_SUBSPACES * SUBSPACE_SIZE), ROW_CHANNELS ** -0.5, 0.375, ((1, 4),)),
        "scoring_final_matrix": scatter_about(splits[6], (NUM_SUBSPACES * SUBSPACE_SIZE, ROW_CHANNELS), (NUM_SUBSPACES * SUBSPACE_SIZE) ** -0.5, 0.375, ((0, 4),)),
        "couple_offset_matrix": draw_couple_offset_matrix(jax.random.fold_in(splits[15], 71), 0),
        "product_first_matrix": scatter_about(splits[8], (ROW_CHANNELS, PROJ_CHANNELS), ROW_CHANNELS ** -0.5, 0.375),
        "product_second_matrix": scatter_about(splits[9], (ROW_CHANNELS, PROJ_CHANNELS), ROW_CHANNELS ** -0.5, 0.375),
        "product_final_matrix": scatter_about(splits[10], (PROJ_CHANNELS * PROJ_CHANNELS, CP), PROJ_CHANNELS ** -0.5, 1.0),
        "trio_first_matrix": scatter_about(splits[11], (2, CP, CP), CP ** -0.5, 0.5, ((2, 4),)),
        "trio_second_matrix": scatter_about(splits[12], (2, CP, CP), CP ** -0.5, 0.5, ((2, 4),)),
        "trio_sigmoid_matrix": scatter_about(splits[13], (CP, CP), CP ** -0.5, 0.5),
        "trio_final_matrix": scatter_about(splits[14], (CP, CP), CP ** -0.5, 0.5),
    }


EPS = 1e-05

def standardise_rows(values):
    values = values.astype(jnp.float32)
    centred = values - lax.optimization_barrier(jnp.mean(values, axis=-1, keepdims=True))
    variance = lax.optimization_barrier(jnp.mean(centred * centred, axis=-1, keepdims=True))
    return centred / jnp.sqrt(variance + EPS)

def reference(homolog_tensor, couple_tensor, probe_matrix, lookup_matrix, content_matrix, scoring_sigmoid_matrix, scoring_final_matrix, couple_offset_matrix, product_first_matrix, product_second_matrix, product_final_matrix, trio_first_matrix, trio_second_matrix, trio_sigmoid_matrix, trio_final_matrix):
    standardised_tensor = standardise_rows(homolog_tensor).astype(jnp.bfloat16)
    reshaped_matrix = standardised_tensor.reshape(NUM_HOMOLOGS * NUM_POSITIONS, ROW_CHANNELS)

    def apply_linear(weights):
        return jnp.dot(reshaped_matrix, weights, preferred_element_type=jnp.float32)
    query = apply_linear(probe_matrix).astype(jnp.bfloat16).reshape(NUM_HOMOLOGS, NUM_POSITIONS, NUM_SUBSPACES, SUBSPACE_SIZE)
    key = apply_linear(lookup_matrix).astype(jnp.bfloat16).reshape(NUM_HOMOLOGS, NUM_POSITIONS, NUM_SUBSPACES, SUBSPACE_SIZE)
    value = apply_linear(content_matrix).astype(jnp.bfloat16).reshape(NUM_HOMOLOGS, NUM_POSITIONS, NUM_SUBSPACES, SUBSPACE_SIZE)
    gate_pre = apply_linear(scoring_sigmoid_matrix).reshape(NUM_HOMOLOGS, NUM_POSITIONS, NUM_SUBSPACES, SUBSPACE_SIZE)
    pair_normed = standardise_rows(couple_tensor).astype(jnp.bfloat16)
    pair_bias = jnp.dot(pair_normed.reshape(NUM_POSITIONS * NUM_POSITIONS, CP), couple_offset_matrix, preferred_element_type=jnp.float32)
    pair_bias = pair_bias.astype(jnp.bfloat16).reshape(NUM_POSITIONS, NUM_POSITIONS, NUM_SUBSPACES)
    bias_heads = jnp.transpose(pair_bias, (2, 0, 1)).astype(jnp.float32)
    scale = float(SUBSPACE_SIZE) ** (-0.5)

    def one_row(items):
        row_query, row_key, row_value = items
        scores = jnp.einsum('ihd,jhd->hij', row_query.astype(jnp.float32), row_key.astype(jnp.float32)) * scale
        scores = scores + bias_heads
        top = lax.optimization_barrier(jnp.max(scores, axis=-1, keepdims=True))
        expo = jnp.exp(scores - top)
        total = lax.optimization_barrier(jnp.sum(expo, axis=-1))
        weights = expo.astype(jnp.bfloat16)
        summed = jnp.einsum('hij,jhd->ihd', weights.astype(jnp.float32), row_value.astype(jnp.float32))
        return summed / jnp.transpose(total)[:, :, None]
    attended_values = lax.map(one_row, (query, key, value))
    attended_values = (attended_values * jax.nn.sigmoid(gate_pre)).astype(jnp.bfloat16)
    joined_tensor = jnp.dot(attended_values.reshape(NUM_HOMOLOGS * NUM_POSITIONS, NUM_SUBSPACES * SUBSPACE_SIZE), scoring_final_matrix, preferred_element_type=jnp.float32)
    revised_homolog_matrix = (homolog_tensor.astype(jnp.float32) + joined_tensor.reshape(NUM_HOMOLOGS, NUM_POSITIONS, ROW_CHANNELS)).astype(jnp.bfloat16)
    left_outer = apply_linear(product_first_matrix).astype(jnp.bfloat16).reshape(NUM_HOMOLOGS, NUM_POSITIONS, PROJ_CHANNELS)
    right_outer = apply_linear(product_second_matrix).astype(jnp.bfloat16).reshape(NUM_HOMOLOGS, NUM_POSITIONS, PROJ_CHANNELS)
    wide_out = product_final_matrix.astype(jnp.float32)

    def outer_block(piece):
        outer = jnp.einsum('sip,sjq->ijpq', piece.astype(jnp.float32), right_outer.astype(jnp.float32))
        return jnp.dot(outer.reshape(16 * NUM_POSITIONS, PROJ_CHANNELS * PROJ_CHANNELS), wide_out, precision=lax.Precision.HIGHEST).reshape(16, NUM_POSITIONS, CP)
    pieces = jnp.transpose(left_outer.reshape(NUM_HOMOLOGS, NUM_POSITIONS // 16, 16, PROJ_CHANNELS), (1, 0, 2, 3))
    outer_update = lax.map(outer_block, pieces).reshape(NUM_POSITIONS, NUM_POSITIONS, CP) / NUM_HOMOLOGS
    pair_mid = (couple_tensor.astype(jnp.float32) + outer_update).astype(jnp.bfloat16)
    tri_normed = standardise_rows(pair_mid).astype(jnp.bfloat16)
    tri_flat = tri_normed.reshape(NUM_POSITIONS * NUM_POSITIONS, CP)

    def gated(weights):
        linear = jnp.dot(tri_flat, weights[0], preferred_element_type=jnp.float32)
        opening = jnp.dot(tri_flat, weights[1], preferred_element_type=jnp.float32)
        return (jax.nn.sigmoid(opening) * linear).astype(jnp.bfloat16).reshape(NUM_POSITIONS, NUM_POSITIONS, CP)
    tri_left = gated(trio_first_matrix)
    tri_right = gated(trio_second_matrix)
    product = jnp.einsum('ikc,jkc->ijc', tri_left.astype(jnp.float32), tri_right.astype(jnp.float32))
    product_normed = standardise_rows(product).astype(jnp.bfloat16)
    closing = jax.nn.sigmoid(jnp.dot(tri_flat, trio_sigmoid_matrix, preferred_element_type=jnp.float32)).reshape(NUM_POSITIONS, NUM_POSITIONS, CP)
    change = jnp.dot(product_normed.reshape(NUM_POSITIONS * NUM_POSITIONS, CP), trio_final_matrix, preferred_element_type=jnp.float32).reshape(NUM_POSITIONS, NUM_POSITIONS, CP)
    pairwise_output = (pair_mid.astype(jnp.float32) + closing * change).astype(jnp.bfloat16)
    return (revised_homolog_matrix, pairwise_output)
```

```python
import jax
import jax.numpy as jnp
from jax import lax
from jax.experimental import pallas as pl
from jax.experimental.pallas import tpu as pltpu
from jax.sharding import PartitionSpec as P

EPS = 1e-05
MESH = pl.DeviceIdType.MESH
BF = jnp.bfloat16
F32 = jnp.float32
NB, NR, NC = 4, 16, 8
HEADS, DEPTH = 2, 32


def standardise(x):
    centred = x - jnp.mean(x, axis=-1, keepdims=True)
    variance = jnp.mean(centred * centred, axis=-1, keepdims=True)
    return centred * lax.rsqrt(variance + EPS)


def mm(a, b):
    return jnp.dot(a, b, preferred_element_type=F32)


def mm_nt(a, b):
    return lax.dot_general(a, b, (((1,), (1,)), ((), ())), preferred_element_type=F32)


def mm_tn(a, b):
    return lax.dot_general(a, b, (((0,), (0,)), ((), ())), preferred_element_type=F32)


def iota(shape, dim):
    return lax.broadcasted_iota(jnp.int32, shape, dim)


def kernel(
    hom,
    coup,
    coup_t,
    w_att,
    w_lr,
    w_fin,
    w_off,
    w_prod,
    w_tri,
    w_close,
    w_change,
    msa_out,
    pair_out,
    l_send, lbuf, r_send, rbuf, xa, b_send, bb1, b2_send, bb2, tw, midbuf,
    tl_send, tlbuf, tr_scr, tr_send, trbuf, tlf, trf, obuf,
    ctx_send, cb, p_send, pbuf, att,
    s_l, s_r, s_x, s_b1, s_b2, s_w, s_mid, s_tl, s_tr, s_o, s_c, s_p,
):
    b = lax.axis_index("branch")
    r = lax.axis_index("row")
    c = lax.axis_index("col")
    active = (b // 2) == (r % 2)
    c_dest = r // 2
    r_src = 2 * c + b // 2
    same_col = c_dest == c

    barrier = pltpu.get_barrier_semaphore()

    def greet(axis, me, size):
        def body(d, _):
            pl.semaphore_signal(
                barrier, inc=1, device_id={axis: (me + d) % size}, device_id_type=MESH
            )
            return 0

        lax.fori_loop(1, size, body, 0)

    greet("row", r, NR)
    greet("col", c, NC)
    greet("branch", b, NB)

    def greet_source(k, _):
        @pl.when(jnp.logical_or(r_src != r, k != c))
        def _():
            pl.semaphore_signal(
                barrier, inc=1, device_id={"row": r_src, "col": k}, device_id_type=MESH
            )

        return 0

    lax.fori_loop(0, NC, greet_source, 0)

    normed = standardise(hom[...].astype(F32)).astype(BF)
    y = mm(normed, w_lr[...])
    row_i = iota((256, 256), 0) % 8
    lane = iota((256, 256), 1)
    pick = (iota((32, 256), 1) // 8 == iota((32, 256), 0)).astype(BF)
    left = jnp.where(lane % 8 == row_i, y[:, :256], 0.0).astype(BF)
    right = jnp.where(lane // 32 == row_i, y[:, 256:], 0.0).astype(BF)
    l_send[...] = mm(pick, left).astype(BF)
    right = mm(pick, right).astype(BF)
    r_send[...] = jnp.where(b % 2 == 0, right[:, :128], right[:, 128:])

    pair_normed = standardise(coup[...].astype(F32)).astype(BF)
    offs = w_off[...]
    off_row = iota((16, 128), 0) % 8
    tile = jnp.zeros((16, 16), F32)
    for i in range(8):
        tile = tile + mm_nt(
            jnp.where(off_row == i, offs, jnp.zeros_like(offs)), pair_normed[16 * i : 16 * i + 16]
        )
    place = (iota((16, 128), 1) == iota((16, 128), 0) + 16 * c).astype(BF)
    b_send[...] = mm(tile.astype(BF), place).astype(BF)

    pl.semaphore_wait(barrier, 25 + jnp.where(active, jnp.where(same_col, 15, 16), 0))

    def send_group(axis, me, size, source, dest, sems):
        def body(d, _):
            peer = (me + d) % size
            pltpu.make_async_remote_copy(
                src_ref=source(peer),
                dst_ref=dest.at[me],
                send_sem=sems.at[0],
                recv_sem=sems.at[1],
                device_id={axis: peer},
                device_id_type=MESH,
            ).start()
            return 0

        lax.fori_loop(1, size, body, 0)

    def send_right(source, dest, sems):
        @pl.when(active)
        def _():
            def body(peer, _):
                @pl.when(jnp.logical_or(peer != r, jnp.logical_not(same_col)))
                def _():
                    pltpu.make_async_remote_copy(
                        src_ref=source,
                        dst_ref=dest.at[c],
                        send_sem=sems.at[0],
                        recv_sem=sems.at[1],
                        device_id={"row": peer, "col": c_dest},
                        device_id_type=MESH,
                    ).start()

                return 0

            lax.fori_loop(0, NR, body, 0)

            @pl.when(same_col)
            def _():
                pltpu.make_async_copy(source, dest.at[c], sems.at[1]).start()

    def wait_bytes(ref, sem):
        pltpu.make_async_copy(ref, ref, sem).wait()

    def arrived(dest, size, sems):
        wait_bytes(dest.at[pl.ds(0, size)], sems.at[1])

    def left_device(dest, size, sems):
        wait_bytes(dest.at[pl.ds(0, size)], sems.at[0])

    def left_right(dest, sems):
        @pl.when(active)
        def _():
            def body(peer, _):
                @pl.when(jnp.logical_or(peer != r, jnp.logical_not(same_col)))
                def _():
                    wait_bytes(dest.at[0], sems.at[0])

                return 0

            lax.fori_loop(0, NR, body, 0)

    send_group("col", c, NC, lambda peer: l_send, lbuf, s_l)
    send_right(r_send, rbuf, s_r)
    send_group("col", c, NC, lambda peer: b_send, bb1, s_b1)
    send_group("row", r, NR, lambda peer: hom.at[pl.ds(16 * peer, 16)], xa, s_x)
    send_group("branch", b, NB, lambda peer: w_tri, tw, s_w)
    lbuf[c] = l_send[...]
    bb1[c] = b_send[...]
    xa[r] = hom[pl.ds(pl.multiple_of(16 * r, 16), 16), :]
    tw[b] = w_tri[...]

    arrived(bb1, NC - 1, s_b1)
    b2_send[...] = jnp.sum(bb1[...].astype(F32), axis=0).astype(BF)
    send_group("row", r, NR, lambda peer: b2_send, bb2, s_b2)
    bb2[r] = b2_send[...]

    arrived(lbuf, NC - 1, s_l)
    arrived(rbuf, NC, s_r)
    outer = mm_tn(lbuf[...].reshape(256, 256), rbuf[...].reshape(256, 128))
    turned = [outer] + [pltpu.roll(outer, 32 * k, 1) for k in range(1, 4)]
    turned = [t.reshape(8, 4, 8, 128) for t in turned]
    block = iota((8, 8, 128), 2) // 32
    rows = []
    for j in range(4):
        x = jnp.zeros((8, 8, 128), F32)
        for u in range(4):
            x = jnp.where(block == u, turned[(u - j) % 4][:, u], x)
        rows.append(jnp.concatenate([x[t] for t in range(8)], axis=1))
    x = jnp.concatenate(rows, axis=0).astype(BF)
    update = mm(x, w_prod[...]) * (1.0 / 256.0)
    mid = (coup_t[b].astype(F32) + update).astype(BF)
    midbuf[b] = mid
    send_group("branch", b, NB, lambda peer: midbuf.at[b], midbuf, s_mid)
    own_normed = standardise(mid.astype(F32)).astype(BF)
    closing = jax.nn.sigmoid(mm(own_normed, w_close[...]))

    arrived(xa, NR - 1, s_x)
    att[...] = mm(standardise(xa[...].astype(F32).reshape(256, 256)).astype(BF), w_att[...])

    arrived(tw, NB - 1, s_w)
    arrived(midbuf, NB - 1, s_mid)
    tri = standardise(midbuf[...].astype(F32).reshape(128, 128)).astype(BF)

    def tri_linear(kind):
        return mm_nt(tri, tw[:, kind].reshape(128, 128))

    tl_send[...] = (jax.nn.sigmoid(tri_linear(1)) * tri_linear(0)).astype(BF)
    send_group("col", c, NC, lambda peer: tl_send, tlbuf, s_tl)
    tr_scr[...] = jax.nn.sigmoid(tri_linear(3)) * tri_linear(2)
    for jj in range(4):
        tr_send[16 * jj : 16 * jj + 16, :] = tr_scr[
            pl.ds(4 * (b % 2) + jj, 16, stride=8), :
        ].astype(BF)
    send_right(tr_send, trbuf, s_tr)
    tlbuf[c] = tl_send[...]

    arrived(bb2, NR - 1, s_b2)
    bias = bb2[...].astype(F32)
    y4 = att[...].reshape(16, 2, 8, 512)
    head_lane = iota((128, 128), 1) // DEPTH
    contexts = []
    for s in range(2):
        ys = y4[:, s].reshape(128, 512)
        q = ys[:, :128].astype(BF)
        k = ys[:, 128:256].astype(BF)
        v = ys[:, 256:384].astype(BF)
        context = jnp.zeros((128, 128), F32)
        for h in range(HEADS):
            qh = jnp.where(head_lane == h, q, jnp.zeros_like(q))
            scores = mm_nt(qh, k) * (float(DEPTH) ** -0.5)
            scores = scores + bias[:, 8 * h : 8 * h + 8].reshape(128, 128)
            expo = jnp.exp(scores - jnp.max(scores, axis=-1, keepdims=True))
            total = jnp.sum(expo, axis=-1, keepdims=True)
            context = jnp.where(head_lane == h, mm(expo.astype(BF), v) / total, context)
        context = context * jax.nn.sigmoid(ys[:, 384:])
        contexts.append(context.reshape(16, 8, 128))
    ctx_send[...] = jnp.concatenate(contexts, axis=1).astype(BF)
    send_group("row", r, NR, lambda peer: ctx_send.at[peer], cb, s_c)
    cb[r] = ctx_send[r]

    arrived(tlbuf, NC - 1, s_tl)
    arrived(trbuf, NC, s_tr)
    tlf[...] = tlbuf[...].astype(F32)
    trf[...] = trbuf[...].astype(F32)

    def product_step(k, acc):
        acc = list(acc)
        for kk in range(16):
            t = tlf[k, 8 * kk : 8 * kk + 8, :]
            for j in range(4):
                acc[j] = acc[j] + t * trf[k, 16 * j + kk : 16 * j + kk + 1, :]
        return tuple(acc)

    product = lax.fori_loop(
        0, NC, product_step, tuple(jnp.zeros((8, 128), F32) for _ in range(4))
    )
    product_normed = standardise(jnp.concatenate(product, axis=0)).astype(BF)
    change = mm(product_normed, w_change[...])
    obuf[b] = (mid.astype(F32) + closing * change).astype(BF)
    send_group("branch", b, NB, lambda peer: obuf.at[b], obuf, s_o)

    arrived(cb, NR - 1, s_c)
    ctx = cb[...].astype(F32).reshape(256, 128).astype(BF)
    half = iota((16, 8, 128), 2) < 64
    for n in range(NB):
        part = mm(ctx, w_fin[n]).reshape(16, 2, 8, 128)
        p_send[n] = jnp.where(half, part[:, 0], part[:, 1]).reshape(128, 128).astype(BF)
    send_group("branch", b, NB, lambda peer: p_send.at[peer], pbuf, s_p)
    pbuf[b] = p_send[b]
    choose = (iota((256, 128), 0) == 64 * b + iota((256, 128), 1) % 64).astype(BF)
    own = mm(hom[...], choose).reshape(16, 2, 8, 128)
    own = jnp.where(half, own[:, 0], own[:, 1]).reshape(128, 128)

    arrived(obuf, NB - 1, s_o)
    pair_out[...] = obuf[...]
    arrived(pbuf, NB - 1, s_p)
    msa_out[...] = (own + jnp.sum(pbuf[...].astype(F32), axis=0)).astype(BF)

    left_device(lbuf, NC - 1, s_l)
    left_right(rbuf, s_r)
    left_device(bb1, NC - 1, s_b1)
    left_device(xa, NR - 1, s_x)
    left_device(tw, NB - 1, s_w)
    left_device(bb2, NR - 1, s_b2)
    left_device(midbuf, NB - 1, s_mid)
    left_device(tlbuf, NC - 1, s_tl)
    left_right(trbuf, s_tr)
    left_device(cb, NR - 1, s_c)
    left_device(obuf, NB - 1, s_o)
    left_device(pbuf, NB - 1, s_p)


def per_device(
    homolog_tensor,
    couple_tensor,
    probe_matrix,
    lookup_matrix,
    content_matrix,
    scoring_sigmoid_matrix,
    scoring_final_matrix,
    couple_offset_matrix,
    product_first_matrix,
    product_second_matrix,
    product_final_matrix,
    trio_first_matrix,
    trio_second_matrix,
    trio_sigmoid_matrix,
    trio_final_matrix,
):
    hom = homolog_tensor.reshape(256, 256)
    coup = couple_tensor.reshape(128, 128)
    coup_t = jnp.transpose(couple_tensor, (1, 0, 2)).reshape(4, 32, 128)
    w_att = jnp.concatenate(
        [
            jnp.pad(w, ((0, 0), (0, 64)))
            for w in (probe_matrix, lookup_matrix, content_matrix, scoring_sigmoid_matrix)
        ],
        axis=1,
    )
    w_lr = jnp.concatenate(
        [jnp.repeat(product_first_matrix, 8, axis=1), jnp.tile(product_second_matrix, (1, 8))],
        axis=1,
    )
    w_fin = jnp.transpose(scoring_final_matrix.reshape(64, 4, 64), (1, 0, 2))
    w_fin = jnp.pad(jnp.concatenate([w_fin, w_fin], axis=2), ((0, 0), (0, 64), (0, 0)))
    w_off = jnp.repeat(couple_offset_matrix.T, 8, axis=0)
    w_tri = jnp.transpose(jnp.concatenate([trio_first_matrix, trio_second_matrix]), (0, 2, 1))
    vmem = pl.BlockSpec(memory_space=pltpu.VMEM)
    scratch = [
        ((32, 256), BF),
        ((8, 32, 256), BF),
        ((32, 128), BF),
        ((8, 32, 128), BF),
        ((16, 16, 256), BF),
        ((16, 128), BF),
        ((8, 16, 128), BF),
        ((16, 128), BF),
        ((16, 16, 128), BF),
        ((4, 4, 32, 128), BF),
        ((4, 32, 128), BF),
        ((128, 128), BF),
        ((8, 128, 128), BF),
        ((128, 128), F32),
        ((64, 128), BF),
        ((8, 64, 128), BF),
        ((8, 128, 128), F32),
        ((8, 64, 128), F32),
        ((4, 32, 128), BF),
        ((16, 16, 128), BF),
        ((16, 16, 128), BF),
        ((4, 128, 128), BF),
        ((4, 128, 128), BF),
        ((256, 512), F32),
    ]
    msa, pair = pl.pallas_call(
        kernel,
        out_shape=(
            jax.ShapeDtypeStruct((128, 128), BF),
            jax.ShapeDtypeStruct((4, 32, 128), BF),
        ),
        in_specs=[vmem] * 11,
        out_specs=(vmem, vmem),
        scratch_shapes=[pltpu.VMEM(*s) for s in scratch] + [pltpu.SemaphoreType.DMA((2,))] * 12,
        compiler_params=pltpu.CompilerParams(
            collective_id=0, has_side_effects=True, vmem_limit_bytes=32 * 1024 * 1024
        ),
        name="block",
    )(
        hom,
        coup,
        coup_t,
        w_att,
        w_lr,
        w_fin,
        w_off,
        product_final_matrix,
        w_tri,
        trio_sigmoid_matrix,
        trio_final_matrix,
    )
    revised = jnp.transpose(msa.reshape(16, 8, 2, 64), (0, 2, 1, 3)).reshape(32, 8, 64)
    pairwise = jnp.transpose(pair.reshape(16, 8, 128), (1, 0, 2))
    return (revised, pairwise)


def solution(mesh):
    return jax.shard_map(
        per_device,
        mesh=mesh,
        in_specs=(
            P("col", "row", None),
            P("row", "col", None),
            P(None, "branch"),
            P(None, "branch"),
            P(None, "branch"),
            P(None, "branch"),
            P("branch", None),
            P(None, "branch"),
            P(),
            P(),
            P(),
            P(None, None, "branch"),
            P(None, None, "branch"),
            P(),
            P(),
        ),
        out_specs=(P("col", "row", "branch"), P("row", "col", None)),
        check_vma=False,
    )
```

```python
import jax
import jax.numpy as jnp
from jax import lax
from jax.experimental import pallas as pl
from jax.experimental.pallas import tpu as pltpu
from jax.sharding import PartitionSpec as P

EPS = 1e-05
MESH = pl.DeviceIdType.MESH
BF = jnp.bfloat16
F32 = jnp.float32
NB, NR, NC = 4, 16, 8
HEADS, DEPTH = 2, 32


def standardise(x):
    centred = x - jnp.mean(x, axis=-1, keepdims=True)
    variance = jnp.mean(centred * centred, axis=-1, keepdims=True)
    return centred * lax.rsqrt(variance + EPS)


def mm(a, b):
    return jnp.dot(a, b, preferred_element_type=F32)


def mm_nt(a, b):
    return lax.dot_general(a, b, (((1,), (1,)), ((), ())), preferred_element_type=F32)


def mm_tn(a, b):
    return lax.dot_general(a, b, (((0,), (0,)), ((), ())), preferred_element_type=F32)


def iota(shape, dim):
    return lax.broadcasted_iota(jnp.int32, shape, dim)


def kernel(
    hom_hbm,
    coup_hbm,
    wq_hbm, wk_hbm, wv_hbm, wg_hbm,
    wf_hbm,
    wo_hbm,
    wl_hbm, wr_hbm,
    prod_hbm,
    t1_hbm, t2_hbm,
    close_hbm, change_hbm,
    msa_out,
    pair_out,
    hom, coup, wq, wk, wv, wg, wf, wo, wl, wr, w_prod, w_close, w_change,
    l_send, lbuf, r_send, rbuf, xa, b_send, bb1, b2_send, bb2, tw, midbuf, coup_f,
    tl_send, tlbuf, tr_scr, tr_send, trbuf, tlf, trf, obuf,
    ctx_send, cb, p_send, pbuf, aq, ak, av, ag,
    s_in, s_l, s_r, s_x, s_b1, s_b2, s_w, s_mid, s_tl, s_tr, s_o, s_c, s_p,
):
    b = lax.axis_index("branch")
    r = lax.axis_index("row")
    c = lax.axis_index("col")
    active = (b // 2) == (r % 2)
    c_dest = r // 2
    r_src = 2 * c + b // 2
    same_col = c_dest == c

    loads = {
        name: pltpu.make_async_copy(source, dest, s_in.at[n])
        for n, (name, source, dest) in enumerate(
            (
                ("hom", hom_hbm, hom),
                ("wl", wl_hbm, wl),
                ("wr", wr_hbm, wr),
                ("coup", coup_hbm, coup),
                ("wo", wo_hbm, wo),
                ("t1", t1_hbm, tw.at[b, pl.ds(0, 2)]),
                ("t2", t2_hbm, tw.at[b, pl.ds(2, 2)]),
                ("prod", prod_hbm, w_prod),
                ("wq", wq_hbm, wq),
                ("wk", wk_hbm, wk),
                ("wv", wv_hbm, wv),
                ("wg", wg_hbm, wg),
                ("close", close_hbm, w_close),
                ("change", change_hbm, w_change),
                ("wf", wf_hbm, wf),
            )
        )
    }
    for name in loads:
        loads[name].start()

    barrier = pltpu.get_barrier_semaphore()

    def wrapped(value, size):
        return jnp.where(value >= size, value - size, value)

    def greet(axis, me, size):
        def body(d, _):
            pl.semaphore_signal(
                barrier, inc=1, device_id={axis: wrapped(me + d, size)}, device_id_type=MESH
            )
            return 0

        lax.fori_loop(1, size, body, 0)

    greet("row", r, NR)
    greet("col", c, NC)
    greet("branch", b, NB)

    def greet_source(k, _):
        @pl.when(jnp.logical_or(r_src != r, k != c))
        def _():
            pl.semaphore_signal(
                barrier, inc=1, device_id={"row": r_src, "col": k}, device_id_type=MESH
            )

        return 0

    lax.fori_loop(0, NC, greet_source, 0)

    loads["wl"].wait()
    loads["wr"].wait()
    spread = (iota((256, 32), 0) // 8 == iota((256, 32), 1)).astype(BF)
    wl_wide = mm(spread, wl[...]).astype(BF)
    wr_wide = jnp.concatenate([wr[...]] * 8, axis=0)
    row_i = iota((256, 256), 0) % 8
    lane = iota((256, 256), 1)
    pick = (iota((32, 256), 1) // 8 == iota((32, 256), 0)).astype(BF)
    loads["hom"].wait()
    normed = standardise(hom[...].astype(F32)).astype(BF)
    left = jnp.where(lane % 8 == row_i, mm_nt(normed, wl_wide), 0.0).astype(BF)
    right = jnp.where(lane // 32 == row_i, mm_nt(normed, wr_wide), 0.0).astype(BF)
    l_send[...] = mm(pick, left).astype(BF)
    right = mm(pick, right).astype(BF)
    r_send[...] = jnp.where(b % 2 == 0, right[:, :128], right[:, 128:])

    pl.semaphore_wait(barrier, 25 + jnp.where(active, jnp.where(same_col, 15, 16), 0))

    def send_group(axis, me, size, source, dest, sems):
        def body(d, _):
            peer = wrapped(me + d, size)
            pltpu.make_async_remote_copy(
                src_ref=source(peer),
                dst_ref=dest.at[me],
                send_sem=sems.at[0],
                recv_sem=sems.at[1],
                device_id={axis: peer},
                device_id_type=MESH,
            ).start()
            return 0

        lax.fori_loop(1, size, body, 0)

    def send_right(source, dest, sems):
        @pl.when(active)
        def _():
            def body(peer, _):
                @pl.when(jnp.logical_or(peer != r, jnp.logical_not(same_col)))
                def _():
                    pltpu.make_async_remote_copy(
                        src_ref=source,
                        dst_ref=dest.at[c],
                        send_sem=sems.at[0],
                        recv_sem=sems.at[1],
                        device_id={"row": peer, "col": c_dest},
                        device_id_type=MESH,
                    ).start()

                return 0

            lax.fori_loop(0, NR, body, 0)

            @pl.when(same_col)
            def _():
                pltpu.make_async_copy(source, dest.at[c], sems.at[1]).start()

    def wait_bytes(ref, sem):
        pltpu.make_async_copy(ref, ref, sem).wait()

    def arrived(dest, size, sems):
        wait_bytes(dest.at[pl.ds(0, size)], sems.at[1])

    def left_device(dest, size, sems):
        wait_bytes(dest.at[pl.ds(0, size)], sems.at[0])

    def left_right(dest, sems):
        @pl.when(active)
        def _():
            def body(peer, _):
                @pl.when(jnp.logical_or(peer != r, jnp.logical_not(same_col)))
                def _():
                    wait_bytes(dest.at[0], sems.at[0])

                return 0

            lax.fori_loop(0, NR, body, 0)

    send_right(r_send, rbuf, s_r)
    send_group("col", c, NC, lambda peer: l_send, lbuf, s_l)
    lbuf[c] = l_send[...]

    loads["coup"].wait()
    loads["wo"].wait()
    coup_f[...] = coup[...].astype(F32)
    pair_normed = standardise(coup_f[...]).astype(BF)
    heads = wo[...].astype(F32)
    offs = jnp.concatenate(
        [jnp.broadcast_to(heads[h : h + 1], (8, 128)) for h in range(HEADS)], axis=0
    ).astype(BF)
    off_row = iota((16, 128), 0) % 8
    tile = jnp.zeros((16, 16), F32)
    for i in range(8):
        tile = tile + mm_nt(
            jnp.where(off_row == i, offs, jnp.zeros_like(offs)), pair_normed[16 * i : 16 * i + 16]
        )
    place = (iota((16, 128), 1) == iota((16, 128), 0) + 16 * c).astype(BF)
    b_send[...] = mm(tile.astype(BF), place).astype(BF)
    send_group("col", c, NC, lambda peer: b_send, bb1, s_b1)
    bb1[c] = b_send[...]
    send_group("row", r, NR, lambda peer: hom.at[pl.ds(16 * peer, 16)], xa, s_x)
    xa[r] = hom[pl.ds(pl.multiple_of(16 * r, 16), 16), :]
    loads["t1"].wait()
    loads["t2"].wait()
    send_group("branch", b, NB, lambda peer: tw.at[b], tw, s_w)
    coup_own = jnp.concatenate(
        [coup_f[pl.ds(4 * b + j, 8, stride=16), :] for j in range(4)], axis=0
    )

    loads["prod"].wait()
    arrived(lbuf, NC - 1, s_l)
    arrived(rbuf, NC, s_r)
    outer = mm_tn(lbuf[...].reshape(256, 256), rbuf[...].reshape(256, 128))
    turned = [outer] + [pltpu.roll(outer, 32 * k, 1) for k in range(1, 4)]
    turned = [t.reshape(8, 4, 8, 128) for t in turned]
    block = iota((8, 8, 128), 2) // 32
    rows = []
    for j in range(4):
        x = jnp.zeros((8, 8, 128), F32)
        for u in range(4):
            x = jnp.where(block == u, turned[(u - j) % 4][:, u], x)
        rows.append(jnp.concatenate([x[t] for t in range(8)], axis=1))
    x = jnp.concatenate(rows, axis=0).astype(BF)
    update = mm(x, w_prod[...]) * (1.0 / 256.0)
    mid = (coup_own + update).astype(BF)
    midbuf[b] = mid
    send_group("branch", b, NB, lambda peer: midbuf.at[b], midbuf, s_mid)

    arrived(bb1, NC - 1, s_b1)
    b2_send[...] = jnp.sum(bb1[...].astype(F32), axis=0).astype(BF)
    send_group("row", r, NR, lambda peer: b2_send, bb2, s_b2)
    bb2[r] = b2_send[...]

    for name in ("wq", "wk", "wv", "wg"):
        loads[name].wait()
    arrived(xa, NR - 1, s_x)
    att_normed = standardise(xa[...].astype(F32).reshape(256, 256)).astype(BF)

    def by_row(weights, dest):
        y = mm_nt(att_normed, weights).reshape(16, 2, 8, -1)
        for s in range(2):
            dest[s] = y[:, s].reshape(128, -1).astype(dest.dtype)

    by_row(wq[...], aq)
    by_row(wk[...], ak)
    by_row(jnp.concatenate([wv[...]] * 2, axis=0), av)
    by_row(jnp.concatenate([wg[...]] * 2, axis=0), ag)

    arrived(tw, NB - 1, s_w)
    arrived(midbuf, NB - 1, s_mid)
    tri = standardise(midbuf[...].astype(F32).reshape(128, 128)).astype(BF)

    def tri_linear(kind):
        return mm_nt(tri, tw[:, kind].reshape(128, 128))

    tr_scr[...] = jax.nn.sigmoid(tri_linear(3)) * tri_linear(2)
    for jj in range(4):
        tr_send[16 * jj : 16 * jj + 16, :] = tr_scr[
            pl.ds(4 * (b % 2) + jj, 16, stride=8), :
        ].astype(BF)
    send_right(tr_send, trbuf, s_tr)
    tl_send[...] = (jax.nn.sigmoid(tri_linear(1)) * tri_linear(0)).astype(BF)
    send_group("col", c, NC, lambda peer: tl_send, tlbuf, s_tl)
    tlbuf[c] = tl_send[...]

    arrived(bb2, NR - 1, s_b2)
    bias = bb2[...].astype(F32)
    head_lane = iota((128, 64), 1) // DEPTH
    wide_lane = (iota((128, 128), 1) % 64) // DEPTH
    contexts = []
    for s in range(2):
        q = aq[s]
        context = jnp.zeros((128, 128), F32)
        for h in range(HEADS):
            qh = jnp.where(head_lane == h, q, jnp.zeros_like(q))
            scores = mm_nt(qh, ak[s]) * (float(DEPTH) ** -0.5)
            scores = scores + bias[:, 8 * h : 8 * h + 8].reshape(128, 128)
            expo = jnp.exp(scores - jnp.max(scores, axis=-1, keepdims=True))
            total = jnp.sum(expo, axis=-1, keepdims=True)
            context = jnp.where(wide_lane == h, mm(expo.astype(BF), av[s]) / total, context)
        context = context * jax.nn.sigmoid(ag[s])
        contexts.append(context.reshape(16, 8, 128))
    ctx_send[...] = jnp.concatenate(contexts, axis=1).astype(BF)
    send_group("row", r, NR, lambda peer: ctx_send.at[peer], cb, s_c)
    cb[r] = ctx_send[r]

    loads["close"].wait()
    loads["change"].wait()
    loads["wf"].wait()
    own_normed = standardise(mid.astype(F32)).astype(BF)
    closing = jax.nn.sigmoid(mm(own_normed, w_close[...]))
    half = iota((16, 8, 128), 2) < 64
    choose = (iota((256, 128), 0) == 64 * b + iota((256, 128), 1) % 64).astype(BF)
    own = mm(hom[...], choose).reshape(16, 2, 8, 128)
    own = jnp.where(half, own[:, 0], own[:, 1]).reshape(128, 128)

    arrived(cb, NR - 1, s_c)
    ctx = cb[...].astype(F32).reshape(256, 128).astype(BF)
    full = mm(ctx[:, :64], wf[...])
    for n in range(0, NB, 2):
        part = full[:, 64 * n : 64 * n + 128]
        swapped = pltpu.roll(part, 64, 1).reshape(16, 2, 8, 128)
        part = part.reshape(16, 2, 8, 128)
        first = jnp.where(half, part[:, 0], swapped[:, 1])
        second = jnp.where(half, swapped[:, 0], part[:, 1])
        p_send[n] = first.reshape(128, 128).astype(BF)
        p_send[n + 1] = second.reshape(128, 128).astype(BF)
    send_group("branch", b, NB, lambda peer: p_send.at[peer], pbuf, s_p)
    pbuf[b] = p_send[b]

    arrived(tlbuf, NC - 1, s_tl)
    arrived(trbuf, NC, s_tr)
    tlf[...] = tlbuf[...].astype(F32)
    trf[...] = trbuf[...].astype(F32)

    def product_step(k, acc):
        acc = list(acc)
        for kk in range(16):
            t = tlf[k, 8 * kk : 8 * kk + 8, :]
            for j in range(4):
                acc[j] = acc[j] + t * trf[k, 16 * j + kk : 16 * j + kk + 1, :]
        return tuple(acc)

    product = lax.fori_loop(
        0, NC, product_step, tuple(jnp.zeros((8, 128), F32) for _ in range(4))
    )
    product_normed = standardise(jnp.concatenate(product, axis=0)).astype(BF)
    change = mm(product_normed, w_change[...])
    obuf[b] = (mid.astype(F32) + closing * change).astype(BF)
    send_group("branch", b, NB, lambda peer: obuf.at[b], obuf, s_o)

    arrived(pbuf, NB - 1, s_p)
    msa = own + jnp.sum(pbuf[...].astype(F32), axis=0)
    msa_out[:, 0] = msa[:, :64].reshape(16, 8, 64).astype(BF)
    msa_out[:, 1] = pltpu.roll(msa, 64, 1)[:, :64].reshape(16, 8, 64).astype(BF)
    left_device(lbuf, NC - 1, s_l)
    left_right(rbuf, s_r)
    left_device(bb1, NC - 1, s_b1)
    left_device(xa, NR - 1, s_x)
    left_device(tw, NB - 1, s_w)
    left_device(bb2, NR - 1, s_b2)
    left_device(midbuf, NB - 1, s_mid)
    left_device(tlbuf, NC - 1, s_tl)
    left_right(trbuf, s_tr)
    left_device(cb, NR - 1, s_c)
    left_device(pbuf, NB - 1, s_p)
    arrived(obuf, NB - 1, s_o)
    tr_scr[...] = obuf[...].astype(F32).reshape(128, 128)
    for i in range(8):
        pair_out[i] = tr_scr[pl.ds(i, 16, stride=8), :].astype(BF)
    left_device(obuf, NB - 1, s_o)


def per_device(
    homolog_tensor,
    couple_tensor,
    probe_matrix,
    lookup_matrix,
    content_matrix,
    scoring_sigmoid_matrix,
    scoring_final_matrix,
    couple_offset_matrix,
    product_first_matrix,
    product_second_matrix,
    product_final_matrix,
    trio_first_matrix,
    trio_second_matrix,
    trio_sigmoid_matrix,
    trio_final_matrix,
):
    operands = (
        homolog_tensor.reshape(256, 256),
        couple_tensor.reshape(128, 128),
        probe_matrix.T,
        lookup_matrix.T,
        content_matrix.T,
        scoring_sigmoid_matrix.T,
        scoring_final_matrix,
        couple_offset_matrix.T,
        product_first_matrix.T,
        product_second_matrix.T,
        product_final_matrix,
        jnp.transpose(trio_first_matrix, (0, 2, 1)),
        jnp.transpose(trio_second_matrix, (0, 2, 1)),
        trio_sigmoid_matrix,
        trio_final_matrix,
    )
    vmem = pl.BlockSpec(memory_space=pltpu.VMEM)
    scratch = [
        ((256, 256), BF),
        ((128, 128), BF),
        ((64, 256), BF),
        ((64, 256), BF),
        ((64, 256), BF),
        ((64, 256), BF),
        ((64, 256), BF),
        ((2, 128), BF),
        ((32, 256), BF),
        ((32, 256), BF),
        ((1024, 128), BF),
        ((128, 128), BF),
        ((128, 128), BF),
        ((32, 256), BF),
        ((8, 32, 256), BF),
        ((32, 128), BF),
        ((8, 32, 128), BF),
        ((16, 16, 256), BF),
        ((16, 128), BF),
        ((8, 16, 128), BF),
        ((16, 128), BF),
        ((16, 16, 128), BF),
        ((4, 4, 32, 128), BF),
        ((4, 32, 128), BF),
        ((128, 128), F32),
        ((128, 128), BF),
        ((8, 128, 128), BF),
        ((128, 128), F32),
        ((64, 128), BF),
        ((8, 64, 128), BF),
        ((8, 128, 128), F32),
        ((8, 64, 128), F32),
        ((4, 32, 128), BF),
        ((16, 16, 128), BF),
        ((16, 16, 128), BF),
        ((4, 128, 128), BF),
        ((4, 128, 128), BF),
        ((2, 128, 64), BF),
        ((2, 128, 64), BF),
        ((2, 128, 128), BF),
        ((2, 128, 128), F32),
    ]
    msa, pairwise = pl.pallas_call(
        kernel,
        out_shape=(
            jax.ShapeDtypeStruct((16, 2, 8, 64), BF),
            jax.ShapeDtypeStruct((8, 16, 128), BF),
        ),
        in_specs=[pl.BlockSpec(memory_space=pltpu.HBM)] * len(operands),
        out_specs=(vmem, vmem),
        scratch_shapes=[pltpu.VMEM(*s) for s in scratch]
        + [pltpu.SemaphoreType.DMA((len(operands),))]
        + [pltpu.SemaphoreType.DMA((2,))] * 12,
        compiler_params=pltpu.CompilerParams(
            collective_id=0, has_side_effects=True
        ),
        name="block",
    )(*operands)
    return (msa.reshape(32, 8, 64), pairwise)


def solution(mesh):
    return jax.shard_map(
        per_device,
        mesh=mesh,
        in_specs=(
            P("col", "row", None),
            P("row", "col", None),
            P(None, "branch"),
            P(None, "branch"),
            P(None, "branch"),
            P(None, "branch"),
            P("branch", None),
            P(None, "branch"),
            P(),
            P(),
            P(),
            P(None, None, "branch"),
            P(None, None, "branch"),
            P(),
            P(),
        ),
        out_specs=(P("col", "row", "branch"), P("row", "col", None)),
        check_vma=False,
    )
```

```python
import jax
import jax.numpy as jnp
from jax import lax
from jax.experimental import pallas as pl
from jax.experimental.pallas import tpu as pltpu
from jax.sharding import PartitionSpec as P

EPS = 1e-05
MESH = pl.DeviceIdType.MESH
BF = jnp.bfloat16
F32 = jnp.float32
NB, NR, NC = 4, 16, 8
HEADS, DEPTH = 2, 32


def standardise(x):
    centred = x - jnp.mean(x, axis=-1, keepdims=True)
    variance = jnp.mean(centred * centred, axis=-1, keepdims=True)
    return centred * lax.rsqrt(variance + EPS)


def mm(a, b):
    return jnp.dot(a, b, preferred_element_type=F32)


def mm_nt(a, b):
    return lax.dot_general(a, b, (((1,), (1,)), ((), ())), preferred_element_type=F32)


def mm_tn(a, b):
    return lax.dot_general(a, b, (((0,), (0,)), ((), ())), preferred_element_type=F32)


def iota(shape, dim):
    return lax.broadcasted_iota(jnp.int32, shape, dim)


def kernel(
    hom_hbm,
    coup_hbm,
    wq_hbm, wk_hbm, wv_hbm, wg_hbm,
    wf_hbm,
    wo_hbm,
    wl_hbm, wr_hbm,
    prod_hbm,
    t1_hbm, t2_hbm,
    close_hbm, change_hbm,
    msa_out,
    pair_out,
    hom, coup, wq, wk, wv, wg, wf, wo, wl, wr, w_prod, w_close, w_change,
    l_send, lbuf, r_send, rbuf, xa, b_send, bb1, b2_send, bb2, tw, midbuf, coup_f,
    tl_send, tlbuf, tr_scr, tr_send, trbuf, tlf, trf, obuf,
    ctx_send, cb, p_send, pbuf, aq, ak, av, ag,
    s_in, s_l, s_r, s_x, s_b1, s_b2, s_w, s_mid, s_tl, s_tr, s_o, s_c, s_p, s_rd, s_trd,
):
    b = lax.axis_index("branch")
    r = lax.axis_index("row")
    c = lax.axis_index("col")
    active = (b // 2) == (r % 2)
    c_dest = r // 2
    r_src = 2 * c + b // 2
    core = r % 2
    to_core = c % 2
    to_self = jnp.logical_and(c_dest == c, core == to_core)

    loads = {
        name: pltpu.make_async_copy(source, dest, s_in.at[n])
        for n, (name, source, dest) in enumerate(
            (
                ("hom", hom_hbm, hom),
                ("wl", wl_hbm, wl),
                ("wr", wr_hbm, wr),
                ("coup", coup_hbm, coup),
                ("wo", wo_hbm, wo),
                ("t1", t1_hbm, tw.at[b, pl.ds(0, 2)]),
                ("t2", t2_hbm, tw.at[b, pl.ds(2, 2)]),
                ("prod", prod_hbm, w_prod),
                ("wq", wq_hbm, wq),
                ("wk", wk_hbm, wk),
                ("wv", wv_hbm, wv),
                ("wg", wg_hbm, wg),
                ("close", close_hbm, w_close),
                ("change", change_hbm, w_change),
                ("wf", wf_hbm, wf),
            )
        )
    }
    for name in loads:
        loads[name].start()

    barrier = pltpu.get_barrier_semaphore()

    def wrapped(value, size):
        return jnp.where(value >= size, value - size, value)

    def greet(axis, me, size):
        def body(d, _):
            pl.semaphore_signal(
                barrier, inc=1, device_id={axis: wrapped(me + d, size)}, device_id_type=MESH
            )
            return 0

        lax.fori_loop(1, size, body, 0)

    greet("row", r, NR)
    greet("col", c, NC)
    greet("branch", b, NB)

    def greet_source(k, _):
        source_col = 2 * k + core

        @pl.when(jnp.logical_or(r_src != r, source_col != c))
        def _():
            pl.semaphore_signal(
                barrier, inc=1, device_id={"row": r_src, "col": source_col}, device_id_type=MESH
            )

        return 0

    lax.fori_loop(0, NC // 2, greet_source, 0)

    def send_group(axis, me, size, source, dest, sems):
        def body(d, _):
            peer = wrapped(me + d, size)
            pltpu.make_async_remote_copy(
                src_ref=source(peer),
                dst_ref=dest.at[me],
                send_sem=sems.at[0],
                recv_sem=sems.at[1],
                device_id={axis: peer},
                device_id_type=MESH,
            ).start()
            return 0

        lax.fori_loop(1, size, body, 0)

    def for_right(body):
        @pl.when(active)
        def _():
            def step(chip, _):
                peer = 2 * chip + to_core

                @pl.when(jnp.logical_or(peer != r, c_dest != c))
                def _():
                    body(peer)

                return 0

            lax.fori_loop(0, NR // 2, step, 0)

    def send_right(source, dest, sems, direct):
        def send(peer):
            pltpu.make_async_remote_copy(
                src_ref=source,
                dst_ref=dest.at[c],
                send_sem=sems.at[2],
                recv_sem=direct.at[c],
                device_id={"row": peer, "col": c_dest},
                device_id_type=MESH,
            ).start()

        for_right(send)

        @pl.when(jnp.logical_and(active, to_self))
        def _():
            pltpu.make_async_copy(source, dest.at[c], direct.at[c]).start()

    def forward_right(dest, sems, direct):
        def step(k, _):
            block = 2 * k + core
            wait_bytes(dest.at[block], direct.at[block])
            pltpu.make_async_remote_copy(
                src_ref=dest.at[block],
                dst_ref=dest.at[block],
                send_sem=sems.at[0],
                recv_sem=sems.at[1],
                device_id={"row": r + 1 - 2 * core},
                device_id_type=MESH,
            ).start()
            return 0

        lax.fori_loop(0, NC // 2, step, 0)

    def wait_bytes(ref, sem):
        pltpu.make_async_copy(ref, ref, sem).wait()

    def arrived(dest, size, sems):
        wait_bytes(dest.at[pl.ds(0, size)], sems.at[1])

    def left_device(dest, size, sems):
        wait_bytes(dest.at[pl.ds(0, size)], sems.at[0])

    def left_right(dest, sems):
        left_device(dest, NC // 2, sems)
        for_right(lambda peer: wait_bytes(dest.at[0], sems.at[2]))

    loads["wl"].wait()
    loads["wr"].wait()
    spread = (iota((256, 32), 0) // 8 == iota((256, 32), 1)).astype(BF)
    wl_wide = mm(spread, wl[...]).astype(BF)
    wr_wide = jnp.concatenate([wr[...]] * 8, axis=0)
    row_i = iota((256, 256), 0) % 8
    lane = iota((256, 256), 1)
    pick = (iota((32, 256), 1) // 8 == iota((32, 256), 0)).astype(BF)

    pl.semaphore_wait(barrier, 25 + jnp.where(active, jnp.where(to_self, 7, 8), 0))
    send_group("row", r, NR, lambda peer: hom_hbm.at[pl.ds(16 * peer, 16)], xa, s_x)
    loads["hom"].wait()
    normed = standardise(hom[...].astype(F32)).astype(BF)
    left = jnp.where(lane % 8 == row_i, mm_nt(normed, wl_wide), 0.0).astype(BF)
    right = jnp.where(lane // 32 == row_i, mm_nt(normed, wr_wide), 0.0).astype(BF)
    l_send[...] = mm(pick, left).astype(BF)
    right = mm(pick, right).astype(BF)
    r_send[...] = jnp.where(b % 2 == 0, right[:, :128], right[:, 128:])

    send_right(r_send, rbuf, s_r, s_rd)
    send_group("col", c, NC, lambda peer: l_send, lbuf, s_l)
    lbuf[c] = l_send[...]
    xa[r] = hom[pl.ds(pl.multiple_of(16 * r, 16), 16), :]
    loads["t1"].wait()
    loads["t2"].wait()
    send_group("branch", b, NB, lambda peer: tw.at[b], tw, s_w)

    loads["coup"].wait()
    loads["wo"].wait()
    coup_f[...] = coup[...].astype(F32)
    pair_normed = standardise(coup_f[...]).astype(BF)
    heads = wo[...].astype(F32)
    offs = jnp.concatenate(
        [jnp.broadcast_to(heads[h : h + 1], (8, 128)) for h in range(HEADS)], axis=0
    ).astype(BF)
    off_row = iota((16, 128), 0) % 8
    tile = jnp.zeros((16, 16), F32)
    for i in range(8):
        tile = tile + mm_nt(
            jnp.where(off_row == i, offs, jnp.zeros_like(offs)), pair_normed[16 * i : 16 * i + 16]
        )
    place = (iota((16, 128), 1) == iota((16, 128), 0) + 16 * c).astype(BF)
    b_send[...] = mm(tile.astype(BF), place).astype(BF)
    send_group("col", c, NC, lambda peer: b_send, bb1, s_b1)
    bb1[c] = b_send[...]
    coup_own = jnp.concatenate(
        [coup_f[pl.ds(4 * b + j, 8, stride=16), :] for j in range(4)], axis=0
    )

    for name in ("wq", "wk", "wv", "wg"):
        loads[name].wait()
    arrived(xa, NR - 1, s_x)
    att_normed = standardise(xa[...].astype(F32).reshape(256, 256)).astype(BF)

    def by_row(weights, dest):
        y = mm_nt(att_normed, weights).reshape(16, 2, 8, -1)
        for s in range(2):
            dest[s] = y[:, s].reshape(128, -1).astype(dest.dtype)

    by_row(wq[...], aq)
    by_row(wk[...], ak)
    by_row(jnp.concatenate([wv[...]] * 2, axis=0), av)
    by_row(jnp.concatenate([wg[...]] * 2, axis=0), ag)

    arrived(bb1, NC - 1, s_b1)
    b2_send[...] = jnp.sum(bb1[...].astype(F32), axis=0).astype(BF)
    send_group("row", r, NR, lambda peer: b2_send, bb2, s_b2)
    bb2[r] = b2_send[...]

    loads["prod"].wait()
    arrived(lbuf, NC - 1, s_l)
    forward_right(rbuf, s_r, s_rd)
    arrived(rbuf, NC // 2, s_r)
    outer = mm_tn(lbuf[...].reshape(256, 256), rbuf[...].reshape(256, 128))
    turned = [outer] + [pltpu.roll(outer, 32 * k, 1) for k in range(1, 4)]
    turned = [t.reshape(8, 4, 8, 128) for t in turned]
    block = iota((8, 8, 128), 2) // 32
    rows = []
    for j in range(4):
        x = jnp.zeros((8, 8, 128), F32)
        for u in range(4):
            x = jnp.where(block == u, turned[(u - j) % 4][:, u], x)
        rows.append(jnp.concatenate([x[t] for t in range(8)], axis=1))
    x = jnp.concatenate(rows, axis=0).astype(BF)
    update = mm(x, w_prod[...]) * (1.0 / 256.0)
    mid = (coup_own + update).astype(BF)
    midbuf[b] = mid
    send_group("branch", b, NB, lambda peer: midbuf.at[b], midbuf, s_mid)

    arrived(bb2, NR - 1, s_b2)
    bias = bb2[...].astype(F32)
    head_lane = iota((128, 64), 1) // DEPTH
    wide_lane = (iota((128, 128), 1) % 64) // DEPTH
    contexts = []
    for s in range(2):
        q = aq[s]
        context = jnp.zeros((128, 128), F32)
        for h in range(HEADS):
            qh = jnp.where(head_lane == h, q, jnp.zeros_like(q))
            scores = mm_nt(qh, ak[s]) * (float(DEPTH) ** -0.5)
            scores = scores + bias[:, 8 * h : 8 * h + 8].reshape(128, 128)
            expo = jnp.exp(scores - jnp.max(scores, axis=-1, keepdims=True))
            total = jnp.sum(expo, axis=-1, keepdims=True)
            context = jnp.where(wide_lane == h, mm(expo.astype(BF), av[s]) / total, context)
        context = context * jax.nn.sigmoid(ag[s])
        contexts.append(context.reshape(16, 8, 128))
    ctx_send[...] = jnp.concatenate(contexts, axis=1).astype(BF)
    send_group("row", r, NR, lambda peer: ctx_send.at[peer], cb, s_c)
    cb[r] = ctx_send[r]

    arrived(tw, NB - 1, s_w)
    arrived(midbuf, NB - 1, s_mid)
    tri = standardise(midbuf[...].astype(F32).reshape(128, 128)).astype(BF)

    def tri_linear(kind):
        return mm_nt(tri, tw[:, kind].reshape(128, 128))

    tr_scr[...] = jax.nn.sigmoid(tri_linear(3)) * tri_linear(2)
    for jj in range(4):
        tr_send[16 * jj : 16 * jj + 16, :] = tr_scr[
            pl.ds(4 * (b % 2) + jj, 16, stride=8), :
        ].astype(BF)
    send_right(tr_send, trbuf, s_tr, s_trd)
    tl_send[...] = (jax.nn.sigmoid(tri_linear(1)) * tri_linear(0)).astype(BF)
    send_group("col", c, NC, lambda peer: tl_send, tlbuf, s_tl)
    tlbuf[c] = tl_send[...]

    loads["close"].wait()
    loads["change"].wait()
    loads["wf"].wait()
    own_normed = standardise(mid.astype(F32)).astype(BF)
    closing = jax.nn.sigmoid(mm(own_normed, w_close[...]))
    half = iota((16, 8, 128), 2) < 64
    choose = (iota((256, 128), 0) == 64 * b + iota((256, 128), 1) % 64).astype(BF)
    own = mm(hom[...], choose).reshape(16, 2, 8, 128)
    own = jnp.where(half, own[:, 0], own[:, 1]).reshape(128, 128)

    arrived(cb, NR - 1, s_c)
    ctx = cb[...].astype(F32).reshape(256, 128).astype(BF)
    full = mm(ctx[:, :64], wf[...])
    for n in range(0, NB, 2):
        part = full[:, 64 * n : 64 * n + 128]
        swapped = pltpu.roll(part, 64, 1).reshape(16, 2, 8, 128)
        part = part.reshape(16, 2, 8, 128)
        first = jnp.where(half, part[:, 0], swapped[:, 1])
        second = jnp.where(half, swapped[:, 0], part[:, 1])
        p_send[n] = first.reshape(128, 128).astype(BF)
        p_send[n + 1] = second.reshape(128, 128).astype(BF)
    send_group("branch", b, NB, lambda peer: p_send.at[peer], pbuf, s_p)
    pbuf[b] = p_send[b]

    forward_right(trbuf, s_tr, s_trd)
    arrived(tlbuf, NC - 1, s_tl)
    arrived(trbuf, NC // 2, s_tr)
    tlf[...] = tlbuf[...].astype(F32)
    trf[...] = trbuf[...].astype(F32)

    def product_step(k, acc):
        acc = list(acc)
        for kk in range(16):
            t = tlf[k, 8 * kk : 8 * kk + 8, :]
            for j in range(4):
                acc[j] = acc[j] + t * trf[k, 16 * j + kk : 16 * j + kk + 1, :]
        return tuple(acc)

    product = lax.fori_loop(
        0, NC, product_step, tuple(jnp.zeros((8, 128), F32) for _ in range(4))
    )
    product_normed = standardise(jnp.concatenate(product, axis=0)).astype(BF)
    change = mm(product_normed, w_change[...])
    obuf[b] = (mid.astype(F32) + closing * change).astype(BF)
    send_group("branch", b, NB, lambda peer: obuf.at[b], obuf, s_o)

    arrived(pbuf, NB - 1, s_p)
    msa = own + jnp.sum(pbuf[...].astype(F32), axis=0)
    msa_out[:, 0] = msa[:, :64].reshape(16, 8, 64).astype(BF)
    msa_out[:, 1] = pltpu.roll(msa, 64, 1)[:, :64].reshape(16, 8, 64).astype(BF)
    left_device(lbuf, NC - 1, s_l)
    left_right(rbuf, s_r)
    left_device(bb1, NC - 1, s_b1)
    left_device(xa, NR - 1, s_x)
    left_device(tw, NB - 1, s_w)
    left_device(bb2, NR - 1, s_b2)
    left_device(midbuf, NB - 1, s_mid)
    left_device(tlbuf, NC - 1, s_tl)
    left_right(trbuf, s_tr)
    left_device(cb, NR - 1, s_c)
    left_device(pbuf, NB - 1, s_p)
    arrived(obuf, NB - 1, s_o)
    tr_scr[...] = obuf[...].astype(F32).reshape(128, 128)
    for i in range(8):
        pair_out[i] = tr_scr[pl.ds(i, 16, stride=8), :].astype(BF)
    left_device(obuf, NB - 1, s_o)


def per_device(
    homolog_tensor,
    couple_tensor,
    probe_matrix,
    lookup_matrix,
    content_matrix,
    scoring_sigmoid_matrix,
    scoring_final_matrix,
    couple_offset_matrix,
    product_first_matrix,
    product_second_matrix,
    product_final_matrix,
    trio_first_matrix,
    trio_second_matrix,
    trio_sigmoid_matrix,
    trio_final_matrix,
):
    operands = (
        homolog_tensor.reshape(256, 256),
        couple_tensor.reshape(128, 128),
        probe_matrix.T,
        lookup_matrix.T,
        content_matrix.T,
        scoring_sigmoid_matrix.T,
        scoring_final_matrix,
        couple_offset_matrix.T,
        product_first_matrix.T,
        product_second_matrix.T,
        product_final_matrix,
        jnp.transpose(trio_first_matrix, (0, 2, 1)),
        jnp.transpose(trio_second_matrix, (0, 2, 1)),
        trio_sigmoid_matrix,
        trio_final_matrix,
    )
    vmem = pl.BlockSpec(memory_space=pltpu.VMEM)
    scratch = [
        ((256, 256), BF),
        ((128, 128), BF),
        ((64, 256), BF),
        ((64, 256), BF),
        ((64, 256), BF),
        ((64, 256), BF),
        ((64, 256), BF),
        ((2, 128), BF),
        ((32, 256), BF),
        ((32, 256), BF),
        ((1024, 128), BF),
        ((128, 128), BF),
        ((128, 128), BF),
        ((32, 256), BF),
        ((8, 32, 256), BF),
        ((32, 128), BF),
        ((8, 32, 128), BF),
        ((16, 16, 256), BF),
        ((16, 128), BF),
        ((8, 16, 128), BF),
        ((16, 128), BF),
        ((16, 16, 128), BF),
        ((4, 4, 32, 128), BF),
        ((4, 32, 128), BF),
        ((128, 128), F32),
        ((128, 128), BF),
        ((8, 128, 128), BF),
        ((128, 128), F32),
        ((64, 128), BF),
        ((8, 64, 128), BF),
        ((8, 128, 128), F32),
        ((8, 64, 128), F32),
        ((4, 32, 128), BF),
        ((16, 16, 128), BF),
        ((16, 16, 128), BF),
        ((4, 128, 128), BF),
        ((4, 128, 128), BF),
        ((2, 128, 64), BF),
        ((2, 128, 64), BF),
        ((2, 128, 128), BF),
        ((2, 128, 128), F32),
    ]
    msa, pairwise = pl.pallas_call(
        kernel,
        out_shape=(
            jax.ShapeDtypeStruct((16, 2, 8, 64), BF),
            jax.ShapeDtypeStruct((8, 16, 128), BF),
        ),
        in_specs=[pl.BlockSpec(memory_space=pltpu.HBM)] * len(operands),
        out_specs=(vmem, vmem),
        scratch_shapes=[pltpu.VMEM(*s) for s in scratch]
        + [pltpu.SemaphoreType.DMA((len(operands),))]
        + [pltpu.SemaphoreType.DMA((3,))] * 12
        + [pltpu.SemaphoreType.DMA((NC,))] * 2,
        compiler_params=pltpu.CompilerParams(
            collective_id=0, has_side_effects=True
        ),
        name="block",
    )(*operands)
    return (msa.reshape(32, 8, 64), pairwise)


def solution(mesh):
    return jax.shard_map(
        per_device,
        mesh=mesh,
        in_specs=(
            P("col", "row", None),
            P("row", "col", None),
            P(None, "branch"),
            P(None, "branch"),
            P(None, "branch"),
            P(None, "branch"),
            P("branch", None),
            P(None, "branch"),
            P(),
            P(),
            P(),
            P(None, None, "branch"),
            P(None, None, "branch"),
            P(),
            P(),
        ),
        out_specs=(P("col", "row", "branch"), P("row", "col", None)),
        check_vma=False,
    )
```

```python
import jax
import jax.numpy as jnp
from jax import lax
from jax.experimental import pallas as pl
from jax.experimental.pallas import tpu as pltpu
from jax.sharding import PartitionSpec as P

EPS = 1e-05
MESH = pl.DeviceIdType.MESH
BF = jnp.bfloat16
F32 = jnp.float32
NB, NR, NC = 4, 16, 8
HEADS, DEPTH = 2, 32


def standardise(x):
    centred = x - jnp.mean(x, axis=-1, keepdims=True)
    variance = jnp.mean(centred * centred, axis=-1, keepdims=True)
    return centred * lax.rsqrt(variance + EPS)


def mm(a, b):
    return jnp.dot(a, b, preferred_element_type=F32)


def mm_nt(a, b):
    return lax.dot_general(a, b, (((1,), (1,)), ((), ())), preferred_element_type=F32)


def mm_tn(a, b):
    return lax.dot_general(a, b, (((0,), (0,)), ((), ())), preferred_element_type=F32)


def iota(shape, dim):
    return lax.broadcasted_iota(jnp.int32, shape, dim)


def kernel(
    hom_hbm,
    coup_hbm,
    wq_hbm, wk_hbm, wv_hbm, wg_hbm,
    wf_hbm,
    wo_hbm,
    wl_hbm, wr_hbm,
    prod_hbm,
    t1_hbm, t2_hbm,
    close_hbm, change_hbm,
    msa_out,
    pair_out,
    hom, coup, wq, wk, wv, wg, wo, wl, wr, w_prod, w_close, w_change,
    l_send, lbuf, r_send, rbuf, xa, b_send, bb1, b2_send, bb2, tw, wfall, midbuf, coup_f,
    tl_send, tlbuf, tr_send, trbuf, tlf, trf, p_send, pbuf, tile_f,
    ctx_send, cb, aq, ak, av, ag,
    s_in, s_l, s_r, s_x, s_b1, s_b2, s_w, s_wf, s_mid, s_tl, s_tr, s_c, s_p,
):
    b = lax.axis_index("branch")
    r = lax.axis_index("row")
    c = lax.axis_index("col")
    active = (b // 2) == (r % 2)
    c_dest = r // 2
    same_col = c_dest == c

    loads = {
        name: pltpu.make_async_copy(source, dest, s_in.at[n])
        for n, (name, source, dest) in enumerate(
            (
                ("hom", hom_hbm, hom),
                ("wl", wl_hbm, wl),
                ("wr", wr_hbm, wr),
                ("coup", coup_hbm, coup),
                ("wo", wo_hbm, wo),
                ("t1", t1_hbm, tw.at[b, pl.ds(0, 2)]),
                ("t2", t2_hbm, tw.at[b, pl.ds(2, 2)]),
                ("prod", prod_hbm, w_prod),
                ("wq", wq_hbm, wq),
                ("wk", wk_hbm, wk),
                ("wv", wv_hbm, wv),
                ("wg", wg_hbm, wg),
                ("close", close_hbm, w_close),
                ("change", change_hbm, w_change),
                ("wf", wf_hbm, wfall.at[b]),
            )
        )
    }
    barrier = pltpu.get_barrier_semaphore()

    def wrapped(value, size):
        return jnp.where(value >= size, value - size, value)

    def greet(axis, me, size):
        def body(d, _):
            pl.semaphore_signal(
                barrier, inc=1, device_id={axis: wrapped(me + d, size)}, device_id_type=MESH
            )
            return 0

        lax.fori_loop(1, size, body, 0)

    def greet_diagonal(d, _):
        for e in range(1, NB):
            pl.semaphore_signal(
                barrier,
                inc=1,
                device_id={"branch": wrapped(b + e, NB), "row": wrapped(r + d, NR)},
                device_id_type=MESH,
            )
        return 0

    def greet_source(k, _):
        for half in range(2):
            @pl.when(jnp.logical_or(2 * c + half != r, k != c))
            def _():
                pl.semaphore_signal(
                    barrier,
                    inc=1,
                    device_id={"row": 2 * c + half, "col": k},
                    device_id_type=MESH,
                )

        return 0

    loads["hom"].start()
    lax.fori_loop(0, NC, greet_source, 0)
    lax.fori_loop(1, NR, greet_diagonal, 0)
    greet("row", r, NR)
    greet("branch", b, NB)
    greet("col", c, NC)
    for name in list(loads)[1:]:
        loads[name].start()

    loads["wl"].wait()
    loads["wr"].wait()
    spread = (iota((256, 32), 0) // 8 == iota((256, 32), 1)).astype(BF)
    wl_wide = mm(spread, wl[...]).astype(BF)
    wr_wide = jnp.concatenate([wr[...]] * 8, axis=0)
    row_i = iota((256, 256), 0) % 8
    lane = iota((256, 256), 1)
    pick = (iota((32, 256), 1) // 8 == iota((32, 256), 0)).astype(BF)
    loads["hom"].wait()
    normed = standardise(hom[...].astype(F32)).astype(BF)
    left = jnp.where(lane % 8 == row_i, mm_nt(normed, wl_wide), 0.0).astype(BF)
    right = jnp.where(lane // 32 == row_i, mm_nt(normed, wr_wide), 0.0).astype(BF)
    l_send[...] = mm(pick, left).astype(BF)
    right = mm(pick, right).astype(BF)
    r_send[...] = jnp.where(b % 2 == 0, right[:, :128], right[:, 128:])

    pl.semaphore_wait(barrier, 15 + 7 + 3 + 45 + jnp.where(same_col, 15, 16))

    def send_group(axis, me, size, source, dest, sems):
        def body(d, _):
            peer = wrapped(me + d, size)
            pltpu.make_async_remote_copy(
                src_ref=source(peer),
                dst_ref=dest.at[me],
                send_sem=sems.at[0],
                recv_sem=sems.at[1],
                device_id={axis: peer},
                device_id_type=MESH,
            ).start()
            return 0

        lax.fori_loop(1, size, body, 0)

    def for_transposed(body):
        def step(peer, _):
            @pl.when(jnp.logical_or(peer != r, jnp.logical_not(same_col)))
            def _():
                body(peer)

            return 0

        lax.fori_loop(0, NR, step, 0)

    def send_transposed(source, dest, sems):
        def send(peer):
            pltpu.make_async_remote_copy(
                src_ref=source,
                dst_ref=dest,
                send_sem=sems.at[0],
                recv_sem=sems.at[1],
                device_id={"row": peer, "col": c_dest},
                device_id_type=MESH,
            ).start()

        for_transposed(send)

        @pl.when(same_col)
        def _():
            pltpu.make_async_copy(source, dest, sems.at[1]).start()

    def wait_bytes(ref, sem):
        pltpu.make_async_copy(ref, ref, sem).wait()

    def arrived(dest, size, sems):
        wait_bytes(dest.at[pl.ds(0, size)], sems.at[1])

    def left_device(dest, size, sems):
        wait_bytes(dest.at[pl.ds(0, size)], sems.at[0])

    def left_transposed(ref, sems):
        for_transposed(lambda peer: wait_bytes(ref, sems.at[0]))

    @pl.when(active)
    def _():
        send_transposed(r_send, rbuf.at[c], s_r)

    send_group("col", c, NC, lambda peer: l_send, lbuf, s_l)
    lbuf[c] = l_send[...]

    loads["coup"].wait()
    loads["wo"].wait()
    coup_f[...] = coup[...].astype(F32)
    pair_normed = standardise(coup_f[...]).astype(BF)
    heads = wo[...].astype(F32)
    offs = jnp.concatenate(
        [jnp.broadcast_to(heads[h : h + 1], (8, 128)) for h in range(HEADS)], axis=0
    ).astype(BF)
    off_row = iota((16, 128), 0) % 8
    tile = jnp.zeros((16, 16), F32)
    for i in range(8):
        tile = tile + mm_nt(
            jnp.where(off_row == i, offs, jnp.zeros_like(offs)), pair_normed[16 * i : 16 * i + 16]
        )
    place = (iota((16, 128), 1) == iota((16, 128), 0) + 16 * c).astype(BF)
    b_send[...] = mm(tile.astype(BF), place).astype(BF)
    send_group("col", c, NC, lambda peer: b_send, bb1, s_b1)
    bb1[c] = b_send[...]
    send_group("row", r, NR, lambda peer: hom.at[pl.ds(16 * peer, 16)], xa, s_x)
    xa[r] = hom[pl.ds(pl.multiple_of(16 * r, 16), 16), :]
    loads["t1"].wait()
    loads["t2"].wait()
    send_group("branch", b, NB, lambda peer: tw.at[b], tw, s_w)
    loads["wf"].wait()
    send_group("branch", b, NB, lambda peer: wfall.at[b], wfall, s_wf)
    coup_own = jnp.concatenate(
        [coup_f[pl.ds(4 * b + j, 8, stride=16), :] for j in range(4)], axis=0
    )

    loads["prod"].wait()
    arrived(lbuf, NC - 1, s_l)
    arrived(rbuf, NC, s_r)
    outer = mm_tn(lbuf[...].reshape(256, 256), rbuf[...].reshape(256, 128))
    turned = [outer] + [pltpu.roll(outer, 32 * k, 1) for k in range(1, 4)]
    turned = [t.reshape(8, 4, 8, 128) for t in turned]
    block = iota((8, 8, 128), 2) // 32
    rows = []
    for j in range(4):
        x = jnp.zeros((8, 8, 128), F32)
        for u in range(4):
            x = jnp.where(block == u, turned[(u - j) % 4][:, u], x)
        rows.append(jnp.concatenate([x[t] for t in range(8)], axis=1))
    x = jnp.concatenate(rows, axis=0).astype(BF)
    update = mm(x, w_prod[...]) * (1.0 / 256.0)
    mid = (coup_own + update).astype(BF)
    midbuf[b] = mid

    arrived(tw, NB - 1, s_w)
    tri = standardise(mid.astype(F32)).astype(BF)

    def tri_linear(kind):
        return mm_nt(tri, tw[:, kind].reshape(128, 128))

    tr_send[...] = (jax.nn.sigmoid(tri_linear(3)) * tri_linear(2)).astype(BF)
    send_transposed(tr_send, trbuf.at[r % 2, c], s_tr)
    tl_send[...] = (jax.nn.sigmoid(tri_linear(1)) * tri_linear(0)).astype(BF)
    send_group("col", c, NC, lambda peer: tl_send, tlbuf, s_tl)
    tlbuf[c] = tl_send[...]
    send_group("branch", b, NB, lambda peer: midbuf.at[b], midbuf, s_mid)

    arrived(bb1, NC - 1, s_b1)
    b2_send[...] = jnp.sum(bb1[...].astype(F32), axis=0).astype(BF)
    send_group("row", r, NR, lambda peer: b2_send, bb2, s_b2)
    bb2[r] = b2_send[...]

    for name in ("wq", "wk", "wv", "wg"):
        loads[name].wait()
    arrived(xa, NR - 1, s_x)
    att_normed = standardise(xa[...].astype(F32).reshape(256, 256)).astype(BF)

    def by_row(weights, dest):
        y = mm_nt(att_normed, weights).reshape(16, 2, 8, -1)
        for s in range(2):
            dest[s] = y[:, s].reshape(128, -1).astype(dest.dtype)

    by_row(wq[...], aq)
    by_row(wk[...], ak)
    by_row(jnp.concatenate([wv[...]] * 2, axis=0), av)
    by_row(jnp.concatenate([wg[...]] * 2, axis=0), ag)

    arrived(bb2, NR - 1, s_b2)
    bias = bb2[...].astype(F32)
    head_lane = iota((128, 64), 1) // DEPTH
    wide_lane = (iota((128, 128), 1) % 64) // DEPTH
    contexts = []
    for s in range(2):
        q = aq[s]
        context = jnp.zeros((128, 128), F32)
        for h in range(HEADS):
            qh = jnp.where(head_lane == h, q, jnp.zeros_like(q))
            scores = mm_nt(qh, ak[s]) * (float(DEPTH) ** -0.5)
            scores = scores + bias[:, 8 * h : 8 * h + 8].reshape(128, 128)
            expo = jnp.exp(scores - jnp.max(scores, axis=-1, keepdims=True))
            total = jnp.sum(expo, axis=-1, keepdims=True)
            context = jnp.where(wide_lane == h, mm(expo.astype(BF), av[s]) / total, context)
        context = context * jax.nn.sigmoid(ag[s])
        contexts.append(context.reshape(16, 8, 128))
    first_half = iota((16, 8, 128), 2) < 64
    ctx_send[...] = jnp.where(first_half, contexts[0], contexts[1]).astype(BF)

    def send_context(peer_row, peer_branch):
        pltpu.make_async_remote_copy(
            src_ref=ctx_send.at[peer_row],
            dst_ref=cb.at[b, r],
            send_sem=s_c.at[0],
            recv_sem=s_c.at[1],
            device_id={"branch": peer_branch, "row": peer_row},
            device_id_type=MESH,
        ).start()

    def send_contexts(d, _):
        for e in range(1, NB):
            send_context(wrapped(r + d, NR), wrapped(b + e, NB))
        return 0

    def send_own_branch(d, _):
        send_context(wrapped(r + d, NR), b)
        return 0

    lax.fori_loop(0, NR, send_contexts, 0)
    lax.fori_loop(1, NR, send_own_branch, 0)
    pltpu.make_async_copy(ctx_send.at[r], cb.at[b, r], s_c.at[1]).start()

    loads["close"].wait()
    loads["change"].wait()
    arrived(wfall, NB - 1, s_wf)
    arrived(midbuf, NB - 1, s_mid)
    mid_all = midbuf[...].astype(F32).reshape(128, 128)
    closing = jax.nn.sigmoid(mm(standardise(mid_all).astype(BF), w_close[...]))
    choose = (iota((256, 128), 0) == 64 * b + iota((256, 128), 1) % 64).astype(BF)
    w_own = mm(wfall[...].reshape(256, 256), choose)
    lower = iota((64, 128), 1) < 64
    w_final = []
    for n in range(NB):
        w_n = w_own[64 * n : 64 * n + 64]
        w_final += [jnp.where(lower, w_n, 0.0), jnp.where(lower, 0.0, w_n)]
    w_final = jnp.concatenate(w_final, axis=0).astype(BF)
    half = iota((16, 8, 128), 2) < 64
    own = mm(hom[...], choose).reshape(16, 2, 8, 128)
    own = jnp.where(half, own[:, 0], own[:, 1]).reshape(128, 128)

    arrived(tlbuf, NC - 1, s_tl)
    wait_bytes(trbuf, s_tr.at[1])
    tlf[...] = tlbuf[...].astype(F32)
    trf[...] = trbuf[...].astype(F32)

    def product_step(k, acc):
        acc = list(acc)
        for kk in range(4):
            t = tlf[k, 8 * kk : 8 * kk + 8, :]
            for j in range(16):
                row = 8 * kk + j % 8
                acc[j] = acc[j] + t * trf[j // 8, k, row : row + 1, :]
        return tuple(acc)

    product = lax.fori_loop(
        0, NC, product_step, tuple(jnp.zeros((8, 128), F32) for _ in range(16))
    )
    product = jnp.concatenate(product, axis=0)
    p_send[...] = product.astype(BF)
    send_group("branch", b, NB, lambda peer: p_send, pbuf, s_p)
    pbuf[b] = p_send[...]

    wait_bytes(cb, s_c.at[1])
    ctx = cb[...].astype(F32).reshape(4, 128, 128)
    ctx = jnp.concatenate([ctx[n] for n in range(NB)], axis=1).astype(BF)
    msa = own + mm(ctx, w_final)
    msa_out[:, 0] = msa[:, :64].reshape(16, 8, 64).astype(BF)
    msa_out[:, 1] = pltpu.roll(msa, 64, 1)[:, :64].reshape(16, 8, 64).astype(BF)

    left_device(lbuf, NC - 1, s_l)

    @pl.when(active)
    def _():
        left_transposed(r_send, s_r)

    left_device(bb1, NC - 1, s_b1)
    left_device(xa, NR - 1, s_x)
    left_device(tw, NB - 1, s_w)
    left_device(wfall, NB - 1, s_wf)
    left_device(bb2, NR - 1, s_b2)
    left_device(midbuf, NB - 1, s_mid)
    left_device(tlbuf, NC - 1, s_tl)
    left_transposed(tr_send, s_tr)
    for n in range(NB):
        left_device(cb.at[n], NR if n else NR - 1, s_c)

    arrived(pbuf, NB - 1, s_p)
    total = jnp.sum(pbuf[...].astype(F32), axis=0)
    change = mm(standardise(total).astype(BF), w_change[...])
    tile_f[...] = mid_all + closing * change
    for i in range(8):
        pair_out[i] = tile_f[pl.ds(i, 16, stride=8), :].astype(BF)
    left_device(pbuf, NB - 1, s_p)


def per_device(
    homolog_tensor,
    couple_tensor,
    probe_matrix,
    lookup_matrix,
    content_matrix,
    scoring_sigmoid_matrix,
    scoring_final_matrix,
    couple_offset_matrix,
    product_first_matrix,
    product_second_matrix,
    product_final_matrix,
    trio_first_matrix,
    trio_second_matrix,
    trio_sigmoid_matrix,
    trio_final_matrix,
):
    operands = (
        homolog_tensor.reshape(256, 256),
        couple_tensor.reshape(128, 128),
        probe_matrix.T,
        lookup_matrix.T,
        content_matrix.T,
        scoring_sigmoid_matrix.T,
        scoring_final_matrix,
        couple_offset_matrix.T,
        product_first_matrix.T,
        product_second_matrix.T,
        product_final_matrix,
        jnp.transpose(trio_first_matrix, (0, 2, 1)),
        jnp.transpose(trio_second_matrix, (0, 2, 1)),
        trio_sigmoid_matrix,
        trio_final_matrix,
    )
    vmem = pl.BlockSpec(memory_space=pltpu.VMEM)
    scratch = [
        ((256, 256), BF),
        ((128, 128), BF),
        ((64, 256), BF),
        ((64, 256), BF),
        ((64, 256), BF),
        ((64, 256), BF),
        ((2, 128), BF),
        ((32, 256), BF),
        ((32, 256), BF),
        ((1024, 128), BF),
        ((128, 128), BF),
        ((128, 128), BF),
        ((32, 256), BF),
        ((8, 32, 256), BF),
        ((32, 128), BF),
        ((8, 32, 128), BF),
        ((16, 16, 256), BF),
        ((16, 128), BF),
        ((8, 16, 128), BF),
        ((16, 128), BF),
        ((16, 16, 128), BF),
        ((4, 4, 32, 128), BF),
        ((4, 64, 256), BF),
        ((4, 32, 128), BF),
        ((128, 128), F32),
        ((32, 128), BF),
        ((8, 32, 128), BF),
        ((32, 128), BF),
        ((2, 8, 32, 128), BF),
        ((8, 32, 128), F32),
        ((2, 8, 32, 128), F32),
        ((128, 128), BF),
        ((4, 128, 128), BF),
        ((128, 128), F32),
        ((16, 8, 128), BF),
        ((4, 16, 8, 128), BF),
        ((2, 128, 64), BF),
        ((2, 128, 64), BF),
        ((2, 128, 128), BF),
        ((2, 128, 128), F32),
    ]
    msa, pairwise = pl.pallas_call(
        kernel,
        out_shape=(
            jax.ShapeDtypeStruct((16, 2, 8, 64), BF),
            jax.ShapeDtypeStruct((8, 16, 128), BF),
        ),
        in_specs=[pl.BlockSpec(memory_space=pltpu.HBM)] * len(operands),
        out_specs=(vmem, vmem),
        scratch_shapes=[pltpu.VMEM(*s) for s in scratch]
        + [pltpu.SemaphoreType.DMA((len(operands),))]
        + [pltpu.SemaphoreType.DMA((2,))] * 12,
        compiler_params=pltpu.CompilerParams(
            collective_id=0, has_side_effects=True
        ),
        name="block",
    )(*operands)
    return (msa.reshape(32, 8, 64), pairwise)


def solution(mesh):
    return jax.shard_map(
        per_device,
        mesh=mesh,
        in_specs=(
            P("col", "row", None),
            P("row", "col", None),
            P(None, "branch"),
            P(None, "branch"),
            P(None, "branch"),
            P(None, "branch"),
            P("branch", None),
            P(None, "branch"),
            P(),
            P(),
            P(),
            P(None, None, "branch"),
            P(None, None, "branch"),
            P(),
            P(),
        ),
        out_specs=(P("col", "row", "branch"), P("row", "col", None)),
        check_vma=False,
    )
```

```python
import jax
import jax.numpy as jnp
from jax import lax
from jax.experimental import pallas as pl
from jax.experimental.pallas import tpu as pltpu
from jax.sharding import PartitionSpec as P

EPS = 1e-05
MESH = pl.DeviceIdType.MESH
BF = jnp.bfloat16
F32 = jnp.float32
NB, NR, NC = 4, 16, 8
HEADS, DEPTH = 2, 32


def standardise(x):
    centred = x - jnp.mean(x, axis=-1, keepdims=True)
    variance = jnp.mean(centred * centred, axis=-1, keepdims=True)
    return centred * lax.rsqrt(variance + EPS)


def mm(a, b):
    return jnp.dot(a, b, preferred_element_type=F32)


def mm_nt(a, b):
    return lax.dot_general(a, b, (((1,), (1,)), ((), ())), preferred_element_type=F32)


def mm_tn(a, b):
    return lax.dot_general(a, b, (((0,), (0,)), ((), ())), preferred_element_type=F32)


def iota(shape, dim):
    return lax.broadcasted_iota(jnp.int32, shape, dim)


def kernel(
    hom_hbm,
    coup_hbm,
    wq_hbm, wk_hbm, wv_hbm, wg_hbm,
    wf_hbm,
    wo_hbm,
    wl_hbm, wr_hbm,
    prod_hbm,
    t1_hbm, t2_hbm,
    close_hbm, change_hbm,
    msa_out,
    pair_out,
    hom, coup, wq, wk, wv, wg, wo, wl, wr, w_prod, w_close, w_change,
    l_send, lbuf, r_send, rbuf, xa, b_send, bb1, b2_send, bb2, tw, wfall, midbuf, coup_f,
    tl_send, tlbuf, tr_send, trbuf, tlf, trf, p_send, pbuf, tile_f,
    ctx_send, cb, aq, ak, av, ag,
    s_in, s_l, s_r, s_x, s_b1, s_b2, s_w, s_wf, s_mid, s_tl, s_tr, s_c, s_p,
):
    b = lax.axis_index("branch")
    r = lax.axis_index("row")
    c = lax.axis_index("col")
    active = (b // 2) == (r % 2)
    c_dest = r // 2
    same_col = c_dest == c

    loads = {
        name: pltpu.make_async_copy(source, dest, s_in.at[n])
        for n, (name, source, dest) in enumerate(
            (
                ("hom", hom_hbm, hom),
                ("wl", wl_hbm, wl),
                ("wr", wr_hbm, wr),
                ("coup", coup_hbm, coup),
                ("wo", wo_hbm, wo),
                ("t1", t1_hbm, tw.at[b, pl.ds(0, 2)]),
                ("t2", t2_hbm, tw.at[b, pl.ds(2, 2)]),
                ("prod", prod_hbm, w_prod),
                ("wq", wq_hbm, wq),
                ("wk", wk_hbm, wk),
                ("wv", wv_hbm, wv),
                ("wg", wg_hbm, wg),
                ("close", close_hbm, w_close),
                ("change", change_hbm, w_change),
                ("wf", wf_hbm, wfall.at[b]),
            )
        )
    }
    barrier = pltpu.get_barrier_semaphore()

    def wrapped(value, size):
        return jnp.where(value >= size, value - size, value)

    def greet(axis, me, size):
        def body(d, _):
            pl.semaphore_signal(
                barrier, inc=1, device_id={axis: wrapped(me + d, size)}, device_id_type=MESH
            )
            return 0

        lax.fori_loop(1, size, body, 0)

    def greet_source(k, _):
        for half in range(2):
            @pl.when(jnp.logical_or(2 * c + half != r, k != c))
            def _():
                pl.semaphore_signal(
                    barrier,
                    inc=1,
                    device_id={"row": 2 * c + half, "col": k},
                    device_id_type=MESH,
                )

        return 0

    for name in ("hom", "wl", "wr"):
        loads[name].start()
    lax.fori_loop(0, NC, greet_source, 0)
    greet("row", r, NR)
    greet("branch", b, NB)
    greet("col", c, NC)
    for name in list(loads)[3:]:
        loads[name].start()

    loads["wl"].wait()
    loads["wr"].wait()
    spread = (iota((256, 32), 0) // 8 == iota((256, 32), 1)).astype(BF)
    wl_wide = mm(spread, wl[...]).astype(BF)
    wr_wide = jnp.concatenate([wr[...]] * 8, axis=0)
    row_i = iota((256, 256), 0) % 8
    lane = iota((256, 256), 1)
    pick = (iota((32, 256), 1) // 8 == iota((32, 256), 0)).astype(BF)
    loads["hom"].wait()
    normed = standardise(hom[...].astype(F32)).astype(BF)
    left = jnp.where(lane % 8 == row_i, mm_nt(normed, wl_wide), 0.0).astype(BF)
    right = jnp.where(lane // 32 == row_i, mm_nt(normed, wr_wide), 0.0).astype(BF)
    l_send[...] = mm(pick, left).astype(BF)
    right = mm(pick, right).astype(BF)
    r_send[...] = jnp.where(b % 2 == 0, right[:, :128], right[:, 128:])

    pl.semaphore_wait(barrier, 15 + 7 + 3 + jnp.where(same_col, 15, 16))

    def send_group(axis, me, size, source, dest, sems):
        def body(d, _):
            peer = wrapped(me + d, size)
            pltpu.make_async_remote_copy(
                src_ref=source(peer),
                dst_ref=dest.at[me],
                send_sem=sems.at[0],
                recv_sem=sems.at[1],
                device_id={axis: peer},
                device_id_type=MESH,
            ).start()
            return 0

        lax.fori_loop(1, size, body, 0)

    def for_transposed(body):
        def step(peer, _):
            @pl.when(jnp.logical_or(peer != r, jnp.logical_not(same_col)))
            def _():
                body(peer)

            return 0

        lax.fori_loop(0, NR, step, 0)

    def send_transposed(source, dest, sems):
        def send(peer):
            pltpu.make_async_remote_copy(
                src_ref=source,
                dst_ref=dest,
                send_sem=sems.at[0],
                recv_sem=sems.at[1],
                device_id={"row": peer, "col": c_dest},
                device_id_type=MESH,
            ).start()

        for_transposed(send)

        @pl.when(same_col)
        def _():
            pltpu.make_async_copy(source, dest, sems.at[1]).start()

    def wait_bytes(ref, sem):
        pltpu.make_async_copy(ref, ref, sem).wait()

    def arrived(dest, size, sems):
        wait_bytes(dest.at[pl.ds(0, size)], sems.at[1])

    def left_device(dest, size, sems):
        wait_bytes(dest.at[pl.ds(0, size)], sems.at[0])

    def left_transposed(ref, sems):
        for_transposed(lambda peer: wait_bytes(ref, sems.at[0]))

    @pl.when(active)
    def _():
        send_transposed(r_send, rbuf.at[c], s_r)

    send_group("col", c, NC, lambda peer: l_send, lbuf, s_l)
    send_group("row", r, NR, lambda peer: hom.at[pl.ds(16 * peer, 16)], xa, s_x)
    lbuf[c] = l_send[...]

    loads["coup"].wait()
    loads["wo"].wait()
    coup_f[...] = coup[...].astype(F32)
    pair_normed = standardise(coup_f[...]).astype(BF)
    heads = wo[...].astype(F32)
    offs = jnp.concatenate(
        [jnp.broadcast_to(heads[h : h + 1], (8, 128)) for h in range(HEADS)], axis=0
    ).astype(BF)
    off_row = iota((16, 128), 0) % 8
    tile = jnp.zeros((16, 16), F32)
    for i in range(8):
        tile = tile + mm_nt(
            jnp.where(off_row == i, offs, jnp.zeros_like(offs)), pair_normed[16 * i : 16 * i + 16]
        )
    place = (iota((16, 128), 1) == iota((16, 128), 0) + 16 * c).astype(BF)
    b_send[...] = mm(tile.astype(BF), place).astype(BF)
    send_group("col", c, NC, lambda peer: b_send, bb1, s_b1)
    bb1[c] = b_send[...]
    xa[r] = hom[pl.ds(pl.multiple_of(16 * r, 16), 16), :]
    loads["t1"].wait()
    loads["t2"].wait()
    send_group("branch", b, NB, lambda peer: tw.at[b], tw, s_w)
    loads["wf"].wait()
    send_group("branch", b, NB, lambda peer: wfall.at[b], wfall, s_wf)
    coup_own = jnp.concatenate(
        [coup_f[pl.ds(4 * b + j, 8, stride=16), :] for j in range(4)], axis=0
    )

    arrived(bb1, NC - 1, s_b1)
    b2_send[...] = jnp.sum(bb1[...].astype(F32), axis=0).astype(BF)
    send_group("row", r, NR, lambda peer: b2_send, bb2, s_b2)
    bb2[r] = b2_send[...]

    loads["prod"].wait()
    arrived(lbuf, NC - 1, s_l)
    arrived(rbuf, NC, s_r)
    outer = mm_tn(lbuf[...].reshape(256, 256), rbuf[...].reshape(256, 128))
    turned = [outer] + [pltpu.roll(outer, 32 * k, 1) for k in range(1, 4)]
    turned = [t.reshape(8, 4, 8, 128) for t in turned]
    block = iota((8, 8, 128), 2) // 32
    rows = []
    for j in range(4):
        x = jnp.zeros((8, 8, 128), F32)
        for u in range(4):
            x = jnp.where(block == u, turned[(u - j) % 4][:, u], x)
        rows.append(jnp.concatenate([x[t] for t in range(8)], axis=1))
    x = jnp.concatenate(rows, axis=0).astype(BF)
    update = mm(x, w_prod[...]) * (1.0 / 256.0)
    mid = (coup_own + update).astype(BF)
    midbuf[b] = mid

    arrived(tw, NB - 1, s_w)
    tri = standardise(mid.astype(F32)).astype(BF)

    def tri_linear(kind):
        return mm_nt(tri, tw[:, kind].reshape(128, 128))

    tr_send[...] = (jax.nn.sigmoid(tri_linear(3)) * tri_linear(2)).astype(BF)
    send_transposed(tr_send, trbuf.at[r % 2, c], s_tr)
    tl_send[...] = (jax.nn.sigmoid(tri_linear(1)) * tri_linear(0)).astype(BF)
    send_group("col", c, NC, lambda peer: tl_send, tlbuf, s_tl)
    tlbuf[c] = tl_send[...]
    send_group("branch", b, NB, lambda peer: midbuf.at[b], midbuf, s_mid)

    for name in ("wq", "wk", "wv", "wg"):
        loads[name].wait()
    arrived(xa, NR - 1, s_x)
    att_normed = standardise(xa[...].astype(F32).reshape(256, 256)).astype(BF)

    def by_row(weights, dest):
        y = mm_nt(att_normed, weights).reshape(16, 2, 8, -1)
        for s in range(2):
            dest[s] = y[:, s].reshape(128, -1).astype(dest.dtype)

    by_row(wq[...], aq)
    by_row(wk[...], ak)
    by_row(jnp.concatenate([wv[...]] * 2, axis=0), av)
    by_row(jnp.concatenate([wg[...]] * 2, axis=0), ag)

    arrived(bb2, NR - 1, s_b2)
    bias = bb2[...].astype(F32)
    head_lane = iota((128, 64), 1) // DEPTH
    wide_lane = (iota((128, 128), 1) % 64) // DEPTH
    contexts = []
    for s in range(2):
        q = aq[s]
        context = jnp.zeros((128, 128), F32)
        for h in range(HEADS):
            qh = jnp.where(head_lane == h, q, jnp.zeros_like(q))
            scores = mm_nt(qh, ak[s]) * (float(DEPTH) ** -0.5)
            scores = scores + bias[:, 8 * h : 8 * h + 8].reshape(128, 128)
            expo = jnp.exp(scores - jnp.max(scores, axis=-1, keepdims=True))
            total = jnp.sum(expo, axis=-1, keepdims=True)
            context = jnp.where(wide_lane == h, mm(expo.astype(BF), av[s]) / total, context)
        context = context * jax.nn.sigmoid(ag[s])
        contexts.append(context.reshape(16, 8, 128))
    first_half = iota((16, 8, 128), 2) < 64
    ctx_send[...] = jnp.where(first_half, contexts[0], contexts[1]).astype(BF)

    def send_context(peer_row, peer_branch):
        pltpu.make_async_remote_copy(
            src_ref=ctx_send.at[peer_row],
            dst_ref=cb.at[b, r],
            send_sem=s_c.at[0],
            recv_sem=s_c.at[1],
            device_id={"branch": peer_branch, "row": peer_row},
            device_id_type=MESH,
        ).start()

    def send_contexts(d, _):
        for e in range(1, NB):
            send_context(wrapped(r + d, NR), wrapped(b + e, NB))
        return 0

    def send_own_branch(d, _):
        send_context(wrapped(r + d, NR), b)
        return 0

    lax.fori_loop(0, NR, send_contexts, 0)
    lax.fori_loop(1, NR, send_own_branch, 0)
    pltpu.make_async_copy(ctx_send.at[r], cb.at[b, r], s_c.at[1]).start()

    loads["close"].wait()
    loads["change"].wait()
    arrived(wfall, NB - 1, s_wf)
    arrived(midbuf, NB - 1, s_mid)
    mid_all = midbuf[...].astype(F32).reshape(128, 128)
    closing = jax.nn.sigmoid(mm(standardise(mid_all).astype(BF), w_close[...]))
    choose = (iota((256, 128), 0) == 64 * b + iota((256, 128), 1) % 64).astype(BF)
    w_own = mm(wfall[...].reshape(256, 256), choose)
    lower = iota((64, 128), 1) < 64
    w_final = []
    for n in range(NB):
        w_n = w_own[64 * n : 64 * n + 64]
        w_final += [jnp.where(lower, w_n, 0.0), jnp.where(lower, 0.0, w_n)]
    w_final = jnp.concatenate(w_final, axis=0).astype(BF)
    half = iota((16, 8, 128), 2) < 64
    own = mm(hom[...], choose).reshape(16, 2, 8, 128)
    own = jnp.where(half, own[:, 0], own[:, 1]).reshape(128, 128)

    arrived(tlbuf, NC - 1, s_tl)
    wait_bytes(trbuf, s_tr.at[1])
    tlf[...] = tlbuf[...].astype(F32)
    trf[...] = trbuf[...].astype(F32)

    def product_step(k, acc):
        acc = list(acc)
        for kk in range(4):
            t = tlf[k, 8 * kk : 8 * kk + 8, :]
            for j in range(16):
                row = 8 * kk + j % 8
                acc[j] = acc[j] + t * trf[j // 8, k, row : row + 1, :]
        return tuple(acc)

    product = lax.fori_loop(
        0, NC, product_step, tuple(jnp.zeros((8, 128), F32) for _ in range(16))
    )
    product = jnp.concatenate(product, axis=0)
    p_send[...] = product.astype(BF)
    send_group("branch", b, NB, lambda peer: p_send, pbuf, s_p)
    pbuf[b] = p_send[...]

    wait_bytes(cb, s_c.at[1])
    ctx = cb[...].astype(F32).reshape(4, 128, 128)
    ctx = jnp.concatenate([ctx[n] for n in range(NB)], axis=1).astype(BF)
    msa = own + mm(ctx, w_final)
    msa_out[:, 0] = msa[:, :64].reshape(16, 8, 64).astype(BF)
    msa_out[:, 1] = pltpu.roll(msa, 64, 1)[:, :64].reshape(16, 8, 64).astype(BF)

    left_device(lbuf, NC - 1, s_l)

    @pl.when(active)
    def _():
        left_transposed(r_send, s_r)

    left_device(bb1, NC - 1, s_b1)
    left_device(xa, NR - 1, s_x)
    left_device(tw, NB - 1, s_w)
    left_device(wfall, NB - 1, s_wf)
    left_device(bb2, NR - 1, s_b2)
    left_device(midbuf, NB - 1, s_mid)
    left_device(tlbuf, NC - 1, s_tl)
    left_transposed(tr_send, s_tr)
    for n in range(NB):
        left_device(cb.at[n], NR if n else NR - 1, s_c)

    arrived(pbuf, NB - 1, s_p)
    total = jnp.sum(pbuf[...].astype(F32), axis=0)
    change = mm(standardise(total).astype(BF), w_change[...])
    tile_f[...] = mid_all + closing * change
    for i in range(8):
        pair_out[i] = tile_f[pl.ds(i, 16, stride=8), :].astype(BF)
    left_device(pbuf, NB - 1, s_p)


def per_device(
    homolog_tensor,
    couple_tensor,
    probe_matrix,
    lookup_matrix,
    content_matrix,
    scoring_sigmoid_matrix,
    scoring_final_matrix,
    couple_offset_matrix,
    product_first_matrix,
    product_second_matrix,
    product_final_matrix,
    trio_first_matrix,
    trio_second_matrix,
    trio_sigmoid_matrix,
    trio_final_matrix,
):
    operands = (
        homolog_tensor.reshape(256, 256),
        couple_tensor.reshape(128, 128),
        probe_matrix.T,
        lookup_matrix.T,
        content_matrix.T,
        scoring_sigmoid_matrix.T,
        scoring_final_matrix,
        couple_offset_matrix.T,
        product_first_matrix.T,
        product_second_matrix.T,
        product_final_matrix,
        jnp.transpose(trio_first_matrix, (0, 2, 1)),
        jnp.transpose(trio_second_matrix, (0, 2, 1)),
        trio_sigmoid_matrix,
        trio_final_matrix,
    )
    vmem = pl.BlockSpec(memory_space=pltpu.VMEM)
    scratch = [
        ((256, 256), BF),
        ((128, 128), BF),
        ((64, 256), BF),
        ((64, 256), BF),
        ((64, 256), BF),
        ((64, 256), BF),
        ((2, 128), BF),
        ((32, 256), BF),
        ((32, 256), BF),
        ((1024, 128), BF),
        ((128, 128), BF),
        ((128, 128), BF),
        ((32, 256), BF),
        ((8, 32, 256), BF),
        ((32, 128), BF),
        ((8, 32, 128), BF),
        ((16, 16, 256), BF),
        ((16, 128), BF),
        ((8, 16, 128), BF),
        ((16, 128), BF),
        ((16, 16, 128), BF),
        ((4, 4, 32, 128), BF),
        ((4, 64, 256), BF),
        ((4, 32, 128), BF),
        ((128, 128), F32),
        ((32, 128), BF),
        ((8, 32, 128), BF),
        ((32, 128), BF),
        ((2, 8, 32, 128), BF),
        ((8, 32, 128), F32),
        ((2, 8, 32, 128), F32),
        ((128, 128), BF),
        ((4, 128, 128), BF),
        ((128, 128), F32),
        ((16, 8, 128), BF),
        ((4, 16, 8, 128), BF),
        ((2, 128, 64), BF),
        ((2, 128, 64), BF),
        ((2, 128, 128), BF),
        ((2, 128, 128), F32),
    ]
    msa, pairwise = pl.pallas_call(
        kernel,
        out_shape=(
            jax.ShapeDtypeStruct((16, 2, 8, 64), BF),
            jax.ShapeDtypeStruct((8, 16, 128), BF),
        ),
        in_specs=[pl.BlockSpec(memory_space=pltpu.HBM)] * len(operands),
        out_specs=(vmem, vmem),
        scratch_shapes=[pltpu.VMEM(*s) for s in scratch]
        + [pltpu.SemaphoreType.DMA((len(operands),))]
        + [pltpu.SemaphoreType.DMA((2,))] * 12,
        compiler_params=pltpu.CompilerParams(
            collective_id=0, has_side_effects=True
        ),
        name="block",
    )(*operands)
    return (msa.reshape(32, 8, 64), pairwise)


def solution(mesh):
    return jax.shard_map(
        per_device,
        mesh=mesh,
        in_specs=(
            P("col", "row", None),
            P("row", "col", None),
            P(None, "branch"),
            P(None, "branch"),
            P(None, "branch"),
            P(None, "branch"),
            P("branch", None),
            P(None, "branch"),
            P(),
            P(),
            P(),
            P(None, None, "branch"),
            P(None, None, "branch"),
            P(),
            P(),
        ),
        out_specs=(P("col", "row", "branch"), P("row", "col", None)),
        check_vma=False,
    )
```

```python
import jax
import jax.numpy as jnp
from jax import lax
from jax.experimental import pallas as pl
from jax.experimental.pallas import tpu as pltpu
from jax.sharding import PartitionSpec as P

EPS = 1e-05
MESH = pl.DeviceIdType.MESH
BF = jnp.bfloat16
F32 = jnp.float32
NB, NR, NC = 4, 16, 8
HEADS, DEPTH = 2, 32


def standardise(x):
    centred = x - jnp.mean(x, axis=-1, keepdims=True)
    variance = jnp.mean(centred * centred, axis=-1, keepdims=True)
    return centred * lax.rsqrt(variance + EPS)


def mm(a, b):
    return jnp.dot(a, b, preferred_element_type=F32)


def mm_nt(a, b):
    return lax.dot_general(a, b, (((1,), (1,)), ((), ())), preferred_element_type=F32)


def mm_tn(a, b):
    return lax.dot_general(a, b, (((0,), (0,)), ((), ())), preferred_element_type=F32)


def iota(shape, dim):
    return lax.broadcasted_iota(jnp.int32, shape, dim)


def kernel(
    hom_hbm,
    coup_hbm,
    wq_hbm, wk_hbm, wv_hbm, wg_hbm,
    wf_hbm,
    wo_hbm,
    wl_hbm, wr_hbm,
    prod_hbm,
    t1_hbm, t2_hbm,
    close_hbm, change_hbm,
    msa_out,
    pair_out,
    hom, coup, wq, wk, wv, wg, wo, wl, wr, w_prod, w_close, w_change,
    l_send, lbuf, r_send, rbuf, xa, b_send, bb1, b2_send, bb2, tw, wfall, midbuf, coup_f,
    tl_send, tlbuf, tr_send, trbuf, tlf, trf, p_send, pbuf, tile_f,
    ctx_send, cb, aq, ak, av, ag,
    s_in, s_l, s_r, s_x, s_b1, s_b2, s_w, s_wf, s_mid, s_tl, s_tr, s_c, s_p,
):
    b = lax.axis_index("branch")
    r = lax.axis_index("row")
    c = lax.axis_index("col")
    active = (b // 2) == (r % 2)
    c_dest = r // 2
    same_col = c_dest == c

    loads = {
        name: pltpu.make_async_copy(source, dest, s_in.at[n])
        for n, (name, source, dest) in enumerate(
            (
                ("hom", hom_hbm, hom),
                ("wl", wl_hbm, wl),
                ("wr", wr_hbm, wr),
                ("coup", coup_hbm, coup),
                ("wo", wo_hbm, wo),
                ("t1", t1_hbm, tw.at[b, pl.ds(0, 2)]),
                ("t2", t2_hbm, tw.at[b, pl.ds(2, 2)]),
                ("prod", prod_hbm, w_prod),
                ("wq", wq_hbm, wq),
                ("wk", wk_hbm, wk),
                ("wv", wv_hbm, wv),
                ("wg", wg_hbm, wg),
                ("close", close_hbm, w_close),
                ("change", change_hbm, w_change),
                ("wf", wf_hbm, wfall.at[b]),
            )
        )
    }
    barrier = pltpu.get_barrier_semaphore()

    def wrapped(value, size):
        return jnp.where(value >= size, value - size, value)

    def greet(axis, me, size):
        def body(d, _):
            pl.semaphore_signal(
                barrier, inc=1, device_id={axis: wrapped(me + d, size)}, device_id_type=MESH
            )
            return 0

        lax.fori_loop(1, size, body, 0)

    def greet_source(k, _):
        for half in range(2):
            @pl.when(jnp.logical_or(2 * c + half != r, k != c))
            def _():
                pl.semaphore_signal(
                    barrier,
                    inc=1,
                    device_id={"row": 2 * c + half, "col": k},
                    device_id_type=MESH,
                )

        return 0

    for name in ("hom", "wl", "wr"):
        loads[name].start()
    lax.fori_loop(0, NC, greet_source, 0)
    greet("row", r, NR)
    greet("branch", b, NB)
    greet("col", c, NC)
    for name in list(loads)[3:]:
        loads[name].start()

    loads["wl"].wait()
    loads["wr"].wait()
    spread = (iota((256, 32), 0) // 8 == iota((256, 32), 1)).astype(BF)
    wl_wide = mm(spread, wl[...]).astype(BF)
    wr_wide = jnp.concatenate([wr[...]] * 8, axis=0)
    row_i = iota((256, 256), 0) % 8
    lane = iota((256, 256), 1)
    pick = (iota((32, 256), 1) // 8 == iota((32, 256), 0)).astype(BF)
    loads["hom"].wait()
    normed = standardise(hom[...].astype(F32)).astype(BF)
    left = jnp.where(lane % 8 == row_i, mm_nt(normed, wl_wide), 0.0).astype(BF)
    right = jnp.where(lane // 32 == row_i, mm_nt(normed, wr_wide), 0.0).astype(BF)
    l_send[...] = mm(pick, left).astype(BF)
    right = mm(pick, right).astype(BF)
    r_send[...] = jnp.where(b % 2 == 0, right[:, :128], right[:, 128:])

    pl.semaphore_wait(barrier, 15 + 7 + 3 + jnp.where(same_col, 15, 16))

    def send_group(axis, me, size, source, dest, sems):
        def body(d, _):
            peer = wrapped(me + d, size)
            pltpu.make_async_remote_copy(
                src_ref=source(peer),
                dst_ref=dest.at[me],
                send_sem=sems.at[0],
                recv_sem=sems.at[1],
                device_id={axis: peer},
                device_id_type=MESH,
            ).start()
            return 0

        lax.fori_loop(1, size, body, 0)

    def for_transposed(body):
        def step(peer, _):
            @pl.when(jnp.logical_or(peer != r, jnp.logical_not(same_col)))
            def _():
                body(peer)

            return 0

        lax.fori_loop(0, NR, step, 0)

    def send_transposed(source, dest, sems):
        def send(peer):
            pltpu.make_async_remote_copy(
                src_ref=source,
                dst_ref=dest,
                send_sem=sems.at[0],
                recv_sem=sems.at[1],
                device_id={"row": peer, "col": c_dest},
                device_id_type=MESH,
            ).start()

        for_transposed(send)

        @pl.when(same_col)
        def _():
            pltpu.make_async_copy(source, dest, sems.at[1]).start()

    def wait_bytes(ref, sem):
        pltpu.make_async_copy(ref, ref, sem).wait()

    def arrived(dest, size, sems):
        wait_bytes(dest.at[pl.ds(0, size)], sems.at[1])

    def left_device(dest, size, sems):
        wait_bytes(dest.at[pl.ds(0, size)], sems.at[0])

    def left_transposed(ref, sems):
        for_transposed(lambda peer: wait_bytes(ref, sems.at[0]))

    @pl.when(active)
    def _():
        send_transposed(r_send, rbuf.at[c], s_r)

    send_group("col", c, NC, lambda peer: l_send, lbuf, s_l)
    send_group("row", r, NR, lambda peer: hom.at[pl.ds(16 * peer, 16)], xa, s_x)
    lbuf[c] = l_send[...]

    loads["coup"].wait()
    loads["wo"].wait()
    coup_f[...] = coup[...].astype(F32)
    pair_normed = standardise(coup_f[...]).astype(BF)
    heads = wo[...].astype(F32)
    offs = jnp.concatenate(
        [jnp.broadcast_to(heads[h : h + 1], (8, 128)) for h in range(HEADS)], axis=0
    ).astype(BF)
    off_row = iota((16, 128), 0) % 8
    tile = jnp.zeros((16, 16), F32)
    for i in range(8):
        tile = tile + mm_nt(
            jnp.where(off_row == i, offs, jnp.zeros_like(offs)), pair_normed[16 * i : 16 * i + 16]
        )
    place = (iota((16, 128), 1) == iota((16, 128), 0) + 16 * c).astype(BF)
    b_send[...] = mm(tile.astype(BF), place).astype(BF)
    send_group("col", c, NC, lambda peer: b_send, bb1, s_b1)
    bb1[c] = b_send[...]
    xa[r] = hom[pl.ds(pl.multiple_of(16 * r, 16), 16), :]
    loads["t1"].wait()
    loads["t2"].wait()
    send_group("branch", b, NB, lambda peer: tw.at[b], tw, s_w)
    loads["wf"].wait()
    send_group("branch", b, NB, lambda peer: wfall.at[b], wfall, s_wf)
    coup_own = jnp.concatenate(
        [coup_f[pl.ds(4 * b + j, 8, stride=16), :] for j in range(4)], axis=0
    )

    arrived(bb1, NC - 1, s_b1)
    b2_send[...] = jnp.sum(bb1[...].astype(F32), axis=0).astype(BF)
    send_group("row", r, NR, lambda peer: b2_send, bb2, s_b2)
    bb2[r] = b2_send[...]

    loads["prod"].wait()
    arrived(lbuf, NC - 1, s_l)
    arrived(rbuf, NC, s_r)
    outer = mm_tn(lbuf[...].reshape(256, 256), rbuf[...].reshape(256, 128))
    turned = [outer] + [pltpu.roll(outer, 32 * k, 1) for k in range(1, 4)]
    turned = [t.reshape(8, 4, 8, 128) for t in turned]
    block = iota((8, 8, 128), 2) // 32
    rows = []
    for j in range(4):
        x = jnp.zeros((8, 8, 128), F32)
        for u in range(4):
            x = jnp.where(block == u, turned[(u - j) % 4][:, u], x)
        rows.append(jnp.concatenate([x[t] for t in range(8)], axis=1))
    x = jnp.concatenate(rows, axis=0).astype(BF)
    update = mm(x, w_prod[...]) * (1.0 / 256.0)
    mid = (coup_own + update).astype(BF)
    midbuf[b] = mid

    arrived(tw, NB - 1, s_w)
    tri = standardise(mid.astype(F32)).astype(BF)

    def tri_linear(kind):
        return mm_nt(tri, tw[:, kind].reshape(128, 128))

    tr_send[...] = (jax.nn.sigmoid(tri_linear(3)) * tri_linear(2)).astype(BF)
    send_transposed(tr_send, trbuf.at[r % 2, c], s_tr)
    tl_send[...] = (jax.nn.sigmoid(tri_linear(1)) * tri_linear(0)).astype(BF)
    send_group("col", c, NC, lambda peer: tl_send, tlbuf, s_tl)
    tlbuf[c] = tl_send[...]
    send_group("branch", b, NB, lambda peer: midbuf.at[b], midbuf, s_mid)

    for name in ("wq", "wk", "wv", "wg"):
        loads[name].wait()
    arrived(xa, NR - 1, s_x)
    att_normed = standardise(xa[...].astype(F32).reshape(256, 256)).astype(BF)

    def by_row(weights, dest):
        y = mm_nt(att_normed, weights).reshape(16, 2, 8, -1)
        for s in range(2):
            dest[s] = y[:, s].reshape(128, -1).astype(dest.dtype)

    by_row(wq[...], aq)
    by_row(wk[...], ak)
    by_row(jnp.concatenate([wv[...]] * 2, axis=0), av)
    by_row(jnp.concatenate([wg[...]] * 2, axis=0), ag)

    arrived(bb2, NR - 1, s_b2)
    bias = bb2[...].astype(F32)
    head_lane = iota((128, 64), 1) // DEPTH
    wide_lane = (iota((128, 128), 1) % 64) // DEPTH
    contexts = []
    for s in range(2):
        q = aq[s]
        context = jnp.zeros((128, 128), F32)
        for h in range(HEADS):
            qh = jnp.where(head_lane == h, q, jnp.zeros_like(q))
            scores = mm_nt(qh, ak[s]) * (float(DEPTH) ** -0.5)
            scores = scores + bias[:, 8 * h : 8 * h + 8].reshape(128, 128)
            expo = jnp.exp(scores - jnp.max(scores, axis=-1, keepdims=True))
            total = jnp.sum(expo, axis=-1, keepdims=True)
            context = jnp.where(wide_lane == h, mm(expo.astype(BF), av[s]) / total, context)
        context = context * jax.nn.sigmoid(ag[s])
        contexts.append(context.reshape(16, 8, 128))
    first_half = iota((16, 8, 128), 2) < 64
    ctx_send[...] = jnp.where(first_half, contexts[0], contexts[1]).astype(BF)

    def send_context(peer_row, peer_branch):
        pltpu.make_async_remote_copy(
            src_ref=ctx_send.at[peer_row],
            dst_ref=cb.at[b, r],
            send_sem=s_c.at[0],
            recv_sem=s_c.at[1],
            device_id={"branch": peer_branch, "row": peer_row},
            device_id_type=MESH,
        ).start()

    def send_contexts(d, _):
        for e in range(1, NB):
            send_context(wrapped(r + d, NR), wrapped(b + e, NB))
        return 0

    def send_own_branch(d, _):
        send_context(wrapped(r + d, NR), b)
        return 0

    lax.fori_loop(0, NR, send_contexts, 0)
    lax.fori_loop(1, NR, send_own_branch, 0)
    pltpu.make_async_copy(ctx_send.at[r], cb.at[b, r], s_c.at[1]).start()

    loads["close"].wait()
    loads["change"].wait()
    arrived(wfall, NB - 1, s_wf)
    arrived(midbuf, NB - 1, s_mid)
    mid_all = midbuf[...].astype(F32).reshape(128, 128)
    closing = jax.nn.sigmoid(mm(standardise(mid_all).astype(BF), w_close[...]))
    choose = (iota((256, 128), 0) == 64 * b + iota((256, 128), 1) % 64).astype(BF)
    w_own = mm(wfall[...].reshape(256, 256), choose)
    lower = iota((64, 128), 1) < 64
    w_final = []
    for n in range(NB):
        w_n = w_own[64 * n : 64 * n + 64]
        w_final += [jnp.where(lower, w_n, 0.0), jnp.where(lower, 0.0, w_n)]
    w_final = jnp.concatenate(w_final, axis=0).astype(BF)
    half = iota((16, 8, 128), 2) < 64
    own = mm(hom[...], choose).reshape(16, 2, 8, 128)
    own = jnp.where(half, own[:, 0], own[:, 1]).reshape(128, 128)

    arrived(tlbuf, NC - 1, s_tl)
    wait_bytes(trbuf, s_tr.at[1])
    tlf[...] = tlbuf[...].astype(F32)
    trf[...] = trbuf[...].astype(F32)

    def product_step(k, acc):
        acc = list(acc)
        for kk in range(4):
            t = tlf[k, 8 * kk : 8 * kk + 8, :]
            for j in range(16):
                row = 8 * kk + j % 8
                acc[j] = acc[j] + t * trf[j // 8, k, row : row + 1, :]
        return tuple(acc)

    product = lax.fori_loop(
        0, NC, product_step, tuple(jnp.zeros((8, 128), F32) for _ in range(16))
    )
    product = jnp.concatenate(product, axis=0)
    p_send[...] = product.astype(BF)
    send_group("branch", b, NB, lambda peer: p_send, pbuf, s_p)
    pbuf[b] = p_send[...]

    wait_bytes(cb, s_c.at[1])
    ctx = cb[...].astype(F32).reshape(4, 128, 128)
    ctx = jnp.concatenate([ctx[n] for n in range(NB)], axis=1).astype(BF)
    msa = own + mm(ctx, w_final)
    msa_out[:, 0] = msa[:, :64].reshape(16, 8, 64).astype(BF)
    msa_out[:, 1] = pltpu.roll(msa, 64, 1)[:, :64].reshape(16, 8, 64).astype(BF)

    left_device(lbuf, NC - 1, s_l)

    @pl.when(active)
    def _():
        left_transposed(r_send, s_r)

    left_device(bb1, NC - 1, s_b1)
    left_device(xa, NR - 1, s_x)
    left_device(tw, NB - 1, s_w)
    left_device(wfall, NB - 1, s_wf)
    left_device(bb2, NR - 1, s_b2)
    left_device(midbuf, NB - 1, s_mid)
    left_device(tlbuf, NC - 1, s_tl)
    left_transposed(tr_send, s_tr)
    for n in range(NB):
        left_device(cb.at[n], NR if n else NR - 1, s_c)

    arrived(pbuf, NB - 1, s_p)
    total = jnp.sum(pbuf[...].astype(F32), axis=0)
    change = mm(standardise(total).astype(BF), w_change[...])
    tile_f[...] = mid_all + closing * change
    for i in range(8):
        pair_out[i] = tile_f[pl.ds(i, 16, stride=8), :].astype(BF)
    left_device(pbuf, NB - 1, s_p)


def hand_over(*arrays):
    def kernel(*refs):
        for n in range(len(arrays)):
            refs[len(arrays) + n][...] = refs[n][...]

    vmem = pl.BlockSpec(memory_space=pltpu.VMEM)
    return pl.pallas_call(
        kernel,
        out_shape=tuple(jax.ShapeDtypeStruct(a.shape, a.dtype) for a in arrays),
        in_specs=[vmem] * len(arrays),
        out_specs=(vmem,) * len(arrays),
        name="hand_over",
    )(*arrays)


def per_device(
    homolog_tensor,
    couple_tensor,
    probe_matrix,
    lookup_matrix,
    content_matrix,
    scoring_sigmoid_matrix,
    scoring_final_matrix,
    couple_offset_matrix,
    product_first_matrix,
    product_second_matrix,
    product_final_matrix,
    trio_first_matrix,
    trio_second_matrix,
    trio_sigmoid_matrix,
    trio_final_matrix,
):
    operands = (
        homolog_tensor.reshape(256, 256),
        couple_tensor.reshape(128, 128),
        probe_matrix.T,
        lookup_matrix.T,
        content_matrix.T,
        scoring_sigmoid_matrix.T,
        scoring_final_matrix,
        couple_offset_matrix.T,
        product_first_matrix.T,
        product_second_matrix.T,
        product_final_matrix,
        jnp.transpose(trio_first_matrix, (0, 2, 1)),
        jnp.transpose(trio_second_matrix, (0, 2, 1)),
        trio_sigmoid_matrix,
        trio_final_matrix,
    )
    vmem = pl.BlockSpec(memory_space=pltpu.VMEM)
    scratch = [
        ((256, 256), BF),
        ((128, 128), BF),
        ((64, 256), BF),
        ((64, 256), BF),
        ((64, 256), BF),
        ((64, 256), BF),
        ((2, 128), BF),
        ((32, 256), BF),
        ((32, 256), BF),
        ((1024, 128), BF),
        ((128, 128), BF),
        ((128, 128), BF),
        ((32, 256), BF),
        ((8, 32, 256), BF),
        ((32, 128), BF),
        ((8, 32, 128), BF),
        ((16, 16, 256), BF),
        ((16, 128), BF),
        ((8, 16, 128), BF),
        ((16, 128), BF),
        ((16, 16, 128), BF),
        ((4, 4, 32, 128), BF),
        ((4, 64, 256), BF),
        ((4, 32, 128), BF),
        ((128, 128), F32),
        ((32, 128), BF),
        ((8, 32, 128), BF),
        ((32, 128), BF),
        ((2, 8, 32, 128), BF),
        ((8, 32, 128), F32),
        ((2, 8, 32, 128), F32),
        ((128, 128), BF),
        ((4, 128, 128), BF),
        ((128, 128), F32),
        ((16, 8, 128), BF),
        ((4, 16, 8, 128), BF),
        ((2, 128, 64), BF),
        ((2, 128, 64), BF),
        ((2, 128, 128), BF),
        ((2, 128, 128), F32),
    ]
    msa, pairwise = pl.pallas_call(
        kernel,
        out_shape=(
            jax.ShapeDtypeStruct((16, 2, 8, 64), BF),
            jax.ShapeDtypeStruct((8, 16, 128), BF),
        ),
        in_specs=[pl.BlockSpec(memory_space=pltpu.HBM)] * len(operands),
        out_specs=(vmem, vmem),
        scratch_shapes=[pltpu.VMEM(*s) for s in scratch]
        + [pltpu.SemaphoreType.DMA((len(operands),))]
        + [pltpu.SemaphoreType.DMA((2,))] * 12,
        compiler_params=pltpu.CompilerParams(
            collective_id=0, has_side_effects=True
        ),
        name="block",
    )(*operands)
    return hand_over(msa.reshape(32, 8, 64), pairwise)


def solution(mesh):
    return jax.shard_map(
        per_device,
        mesh=mesh,
        in_specs=(
            P("col", "row", None),
            P("row", "col", None),
            P(None, "branch"),
            P(None, "branch"),
            P(None, "branch"),
            P(None, "branch"),
            P("branch", None),
            P(None, "branch"),
            P(),
            P(),
            P(),
            P(None, None, "branch"),
            P(None, None, "branch"),
            P(),
            P(),
        ),
        out_specs=(P("col", "row", "branch"), P("row", "col", None)),
        check_vma=False,
    )
```

```python
import jax
import jax.numpy as jnp
from jax import lax
from jax.experimental import pallas as pl
from jax.experimental.pallas import tpu as pltpu
from jax.sharding import PartitionSpec as P

EPS = 1e-05
MESH = pl.DeviceIdType.MESH
BF = jnp.bfloat16
F32 = jnp.float32
NB, NR, NC = 4, 16, 8
HEADS, DEPTH = 2, 32


def standardise(x):
    centred = x - jnp.mean(x, axis=-1, keepdims=True)
    variance = jnp.mean(centred * centred, axis=-1, keepdims=True)
    return centred * lax.rsqrt(variance + EPS)


def mm(a, b):
    return jnp.dot(a, b, preferred_element_type=F32)


def mm_nt(a, b):
    return lax.dot_general(a, b, (((1,), (1,)), ((), ())), preferred_element_type=F32)


def mm_tn(a, b):
    return lax.dot_general(a, b, (((0,), (0,)), ((), ())), preferred_element_type=F32)


def farthest_first(size):
    return sorted(range(size), key=lambda d: -min(d, size - d))


def iota(shape, dim):
    return lax.broadcasted_iota(jnp.int32, shape, dim)


def kernel(
    hom_hbm,
    coup_hbm,
    wq_hbm, wk_hbm, wv_hbm, wg_hbm,
    wf_hbm,
    wo_hbm,
    wl_hbm, wr_hbm,
    prod_hbm,
    t1_hbm, t2_hbm,
    close_hbm, change_hbm,
    msa_out,
    pair_out,
    hom, coup, wq, wk, wv, wg, wo, wl, wr, w_prod, w_close, w_change,
    l_send, lbuf, r_send, rbuf, xa, b_send, bb1, b2_send, bb2, tw, wfall, midbuf, coup_f,
    tl_send, tlbuf, tr_send, trbuf, tlf, trf, p_send, pbuf, tile_f,
    ctx_send, cb, aq, ak, av, ag,
    s_in, s_l, s_r, s_x, s_b1, s_b2, s_w, s_wf, s_mid, s_tl, s_tr, s_c, s_p,
):
    b = lax.axis_index("branch")
    r = lax.axis_index("row")
    c = lax.axis_index("col")
    active = (b // 2) == (r % 2)
    c_dest = r // 2
    same_col = c_dest == c

    loads = {
        name: pltpu.make_async_copy(source, dest, s_in.at[n])
        for n, (name, source, dest) in enumerate(
            (
                ("hom", hom_hbm, hom),
                ("wl", wl_hbm, wl),
                ("wr", wr_hbm, wr),
                ("coup", coup_hbm, coup),
                ("wo", wo_hbm, wo),
                ("t1", t1_hbm, tw.at[b, pl.ds(0, 2)]),
                ("t2", t2_hbm, tw.at[b, pl.ds(2, 2)]),
                ("prod", prod_hbm, w_prod),
                ("wq", wq_hbm, wq),
                ("wk", wk_hbm, wk),
                ("wv", wv_hbm, wv),
                ("wg", wg_hbm, wg),
                ("close", close_hbm, w_close),
                ("change", change_hbm, w_change),
                ("wf", wf_hbm, wfall.at[b]),
            )
        )
    }
    barrier = pltpu.get_barrier_semaphore()

    def wrapped(value, size):
        return jnp.where(value >= size, value - size, value)

    def greet(axis, me, size):
        def body(d, _):
            pl.semaphore_signal(
                barrier, inc=1, device_id={axis: wrapped(me + d, size)}, device_id_type=MESH
            )
            return 0

        lax.fori_loop(1, size, body, 0)

    def greet_source(k, _):
        for half in range(2):
            @pl.when(jnp.logical_or(2 * c + half != r, k != c))
            def _():
                pl.semaphore_signal(
                    barrier,
                    inc=1,
                    device_id={"row": 2 * c + half, "col": k},
                    device_id_type=MESH,
                )

        return 0

    for name in ("hom", "wl", "wr"):
        loads[name].start()
    lax.fori_loop(0, NC, greet_source, 0)
    greet("row", r, NR)
    greet("branch", b, NB)
    greet("col", c, NC)
    for name in list(loads)[3:]:
        loads[name].start()

    loads["wl"].wait()
    loads["wr"].wait()
    spread = (iota((256, 32), 0) // 8 == iota((256, 32), 1)).astype(BF)
    wl_wide = mm(spread, wl[...]).astype(BF)
    wr_wide = jnp.concatenate([wr[...]] * 8, axis=0)
    row_i = iota((256, 256), 0) % 8
    lane = iota((256, 256), 1)
    pick = (iota((32, 256), 1) // 8 == iota((32, 256), 0)).astype(BF)
    loads["hom"].wait()
    normed = standardise(hom[...].astype(F32)).astype(BF)
    left = jnp.where(lane % 8 == row_i, mm_nt(normed, wl_wide), 0.0).astype(BF)
    right = jnp.where(lane // 32 == row_i, mm_nt(normed, wr_wide), 0.0).astype(BF)
    l_send[...] = mm(pick, left).astype(BF)
    right = mm(pick, right).astype(BF)
    r_send[...] = jnp.where(b % 2 == 0, right[:, :128], right[:, 128:])

    pl.semaphore_wait(barrier, 15 + 7 + 3 + jnp.where(same_col, 15, 16))

    def send_group(axis, me, size, source, dest, sems):
        for d in farthest_first(size)[:-1]:
            peer = wrapped(me + d, size)
            pltpu.make_async_remote_copy(
                src_ref=source(peer),
                dst_ref=dest.at[me],
                send_sem=sems.at[0],
                recv_sem=sems.at[1],
                device_id={axis: peer},
                device_id_type=MESH,
            ).start()

    def for_transposed(body):
        for d in farthest_first(NR):
            if d:
                body(wrapped(r + d, NR))
            else:
                pl.when(jnp.logical_not(same_col))(lambda: body(r))

    def send_transposed(source, dest, sems):
        def send(peer):
            pltpu.make_async_remote_copy(
                src_ref=source,
                dst_ref=dest,
                send_sem=sems.at[0],
                recv_sem=sems.at[1],
                device_id={"row": peer, "col": c_dest},
                device_id_type=MESH,
            ).start()

        for_transposed(send)

        @pl.when(same_col)
        def _():
            pltpu.make_async_copy(source, dest, sems.at[1]).start()

    def wait_bytes(ref, sem):
        pltpu.make_async_copy(ref, ref, sem).wait()

    def arrived(dest, size, sems):
        wait_bytes(dest.at[pl.ds(0, size)], sems.at[1])

    def left_device(dest, size, sems):
        wait_bytes(dest.at[pl.ds(0, size)], sems.at[0])

    def left_transposed(ref, sems):
        for_transposed(lambda peer: wait_bytes(ref, sems.at[0]))

    @pl.when(active)
    def _():
        send_transposed(r_send, rbuf.at[c], s_r)

    send_group("col", c, NC, lambda peer: l_send, lbuf, s_l)
    send_group("row", r, NR, lambda peer: hom.at[pl.ds(16 * peer, 16)], xa, s_x)
    lbuf[c] = l_send[...]

    loads["coup"].wait()
    loads["wo"].wait()
    coup_f[...] = coup[...].astype(F32)
    pair_normed = standardise(coup_f[...]).astype(BF)
    heads = wo[...].astype(F32)
    offs = jnp.concatenate(
        [jnp.broadcast_to(heads[h : h + 1], (8, 128)) for h in range(HEADS)], axis=0
    ).astype(BF)
    off_row = iota((16, 128), 0) % 8
    tile = jnp.zeros((16, 16), F32)
    for i in range(8):
        tile = tile + mm_nt(
            jnp.where(off_row == i, offs, jnp.zeros_like(offs)), pair_normed[16 * i : 16 * i + 16]
        )
    place = (iota((16, 128), 1) == iota((16, 128), 0) + 16 * c).astype(BF)
    b_send[...] = mm(tile.astype(BF), place).astype(BF)
    send_group("col", c, NC, lambda peer: b_send, bb1, s_b1)
    bb1[c] = b_send[...]
    xa[r] = hom[pl.ds(pl.multiple_of(16 * r, 16), 16), :]
    loads["t1"].wait()
    loads["t2"].wait()
    send_group("branch", b, NB, lambda peer: tw.at[b], tw, s_w)
    loads["wf"].wait()
    send_group("branch", b, NB, lambda peer: wfall.at[b], wfall, s_wf)
    coup_own = jnp.concatenate(
        [coup_f[pl.ds(4 * b + j, 8, stride=16), :] for j in range(4)], axis=0
    )

    arrived(bb1, NC - 1, s_b1)
    b2_send[...] = jnp.sum(bb1[...].astype(F32), axis=0).astype(BF)
    send_group("row", r, NR, lambda peer: b2_send, bb2, s_b2)
    bb2[r] = b2_send[...]

    loads["prod"].wait()
    arrived(lbuf, NC - 1, s_l)
    arrived(rbuf, NC, s_r)
    outer = mm_tn(lbuf[...].reshape(256, 256), rbuf[...].reshape(256, 128))
    turned = [outer] + [pltpu.roll(outer, 32 * k, 1) for k in range(1, 4)]
    turned = [t.reshape(8, 4, 8, 128) for t in turned]
    block = iota((8, 8, 128), 2) // 32
    rows = []
    for j in range(4):
        x = jnp.zeros((8, 8, 128), F32)
        for u in range(4):
            x = jnp.where(block == u, turned[(u - j) % 4][:, u], x)
        rows.append(jnp.concatenate([x[t] for t in range(8)], axis=1))
    x = jnp.concatenate(rows, axis=0).astype(BF)
    update = mm(x, w_prod[...]) * (1.0 / 256.0)
    mid = (coup_own + update).astype(BF)
    midbuf[b] = mid

    arrived(tw, NB - 1, s_w)
    tri = standardise(mid.astype(F32)).astype(BF)

    def tri_linear(kind):
        return mm_nt(tri, tw[:, kind].reshape(128, 128))

    tr_send[...] = (jax.nn.sigmoid(tri_linear(3)) * tri_linear(2)).astype(BF)
    send_transposed(tr_send, trbuf.at[r % 2, c], s_tr)
    tl_send[...] = (jax.nn.sigmoid(tri_linear(1)) * tri_linear(0)).astype(BF)
    send_group("col", c, NC, lambda peer: tl_send, tlbuf, s_tl)
    tlbuf[c] = tl_send[...]
    send_group("branch", b, NB, lambda peer: midbuf.at[b], midbuf, s_mid)

    for name in ("wq", "wk", "wv", "wg"):
        loads[name].wait()
    arrived(xa, NR - 1, s_x)
    att_normed = standardise(xa[...].astype(F32).reshape(256, 256)).astype(BF)

    def by_row(weights, dest):
        y = mm_nt(att_normed, weights).reshape(16, 2, 8, -1)
        for s in range(2):
            dest[s] = y[:, s].reshape(128, -1).astype(dest.dtype)

    by_row(wq[...], aq)
    by_row(wk[...], ak)
    by_row(jnp.concatenate([wv[...]] * 2, axis=0), av)
    by_row(jnp.concatenate([wg[...]] * 2, axis=0), ag)

    arrived(bb2, NR - 1, s_b2)
    bias = bb2[...].astype(F32)
    head_lane = iota((128, 64), 1) // DEPTH
    wide_lane = (iota((128, 128), 1) % 64) // DEPTH
    contexts = []
    for s in range(2):
        q = aq[s]
        context = jnp.zeros((128, 128), F32)
        for h in range(HEADS):
            qh = jnp.where(head_lane == h, q, jnp.zeros_like(q))
            scores = mm_nt(qh, ak[s]) * (float(DEPTH) ** -0.5)
            scores = scores + bias[:, 8 * h : 8 * h + 8].reshape(128, 128)
            expo = jnp.exp(scores - jnp.max(scores, axis=-1, keepdims=True))
            total = jnp.sum(expo, axis=-1, keepdims=True)
            context = jnp.where(wide_lane == h, mm(expo.astype(BF), av[s]) / total, context)
        context = context * jax.nn.sigmoid(ag[s])
        contexts.append(context.reshape(16, 8, 128))
    first_half = iota((16, 8, 128), 2) < 64
    ctx_send[...] = jnp.where(first_half, contexts[0], contexts[1]).astype(BF)

    def send_context(peer_row, peer_branch):
        pltpu.make_async_remote_copy(
            src_ref=ctx_send.at[peer_row],
            dst_ref=cb.at[b, r],
            send_sem=s_c.at[0],
            recv_sem=s_c.at[1],
            device_id={"branch": peer_branch, "row": peer_row},
            device_id_type=MESH,
        ).start()

    def send_contexts(d, _):
        for e in range(1, NB):
            send_context(wrapped(r + d, NR), wrapped(b + e, NB))
        return 0

    def send_own_branch(d, _):
        send_context(wrapped(r + d, NR), b)
        return 0

    lax.fori_loop(0, NR, send_contexts, 0)
    lax.fori_loop(1, NR, send_own_branch, 0)
    pltpu.make_async_copy(ctx_send.at[r], cb.at[b, r], s_c.at[1]).start()

    loads["close"].wait()
    loads["change"].wait()
    arrived(wfall, NB - 1, s_wf)
    arrived(midbuf, NB - 1, s_mid)
    mid_all = midbuf[...].astype(F32).reshape(128, 128)
    closing = jax.nn.sigmoid(mm(standardise(mid_all).astype(BF), w_close[...]))
    choose = (iota((256, 128), 0) == 64 * b + iota((256, 128), 1) % 64).astype(BF)
    w_own = mm(wfall[...].reshape(256, 256), choose)
    lower = iota((64, 128), 1) < 64
    w_final = []
    for n in range(NB):
        w_n = w_own[64 * n : 64 * n + 64]
        w_final += [jnp.where(lower, w_n, 0.0), jnp.where(lower, 0.0, w_n)]
    w_final = jnp.concatenate(w_final, axis=0).astype(BF)
    half = iota((16, 8, 128), 2) < 64
    own = mm(hom[...], choose).reshape(16, 2, 8, 128)
    own = jnp.where(half, own[:, 0], own[:, 1]).reshape(128, 128)

    arrived(tlbuf, NC - 1, s_tl)
    wait_bytes(trbuf, s_tr.at[1])
    tlf[...] = tlbuf[...].astype(F32)
    trf[...] = trbuf[...].astype(F32)

    for half_j in range(2):

        def product_step(k, acc):
            acc = list(acc)
            for kk in range(4):
                t = tlf[k, 8 * kk : 8 * kk + 8, :]
                for j in range(8):
                    row = 8 * kk + j
                    acc[j] = acc[j] + t * trf[half_j, k, row : row + 1, :]
            return tuple(acc)

        product = lax.fori_loop(
            0, NC, product_step, tuple(jnp.zeros((8, 128), F32) for _ in range(8))
        )
        p_send[half_j] = jnp.concatenate(product, axis=0).astype(BF)
        send_group(
            "branch", b, NB, lambda peer: p_send.at[half_j], pbuf.at[half_j], s_p.at[half_j]
        )
        pbuf[half_j, b] = p_send[half_j]

    wait_bytes(cb, s_c.at[1])
    ctx = cb[...].astype(F32).reshape(4, 128, 128)
    ctx = jnp.concatenate([ctx[n] for n in range(NB)], axis=1).astype(BF)
    msa = own + mm(ctx, w_final)
    msa_out[:, 0] = msa[:, :64].reshape(16, 8, 64).astype(BF)
    msa_out[:, 1] = pltpu.roll(msa, 64, 1)[:, :64].reshape(16, 8, 64).astype(BF)

    left_device(lbuf, NC - 1, s_l)

    @pl.when(active)
    def _():
        left_transposed(r_send, s_r)

    left_device(bb1, NC - 1, s_b1)
    left_device(xa, NR - 1, s_x)
    left_device(tw, NB - 1, s_w)
    left_device(wfall, NB - 1, s_wf)
    left_device(bb2, NR - 1, s_b2)
    left_device(midbuf, NB - 1, s_mid)
    left_device(tlbuf, NC - 1, s_tl)
    left_transposed(tr_send, s_tr)
    for n in range(NB):
        left_device(cb.at[n], NR if n else NR - 1, s_c)

    for half_j in range(2):
        arrived(pbuf.at[half_j], NB - 1, s_p.at[half_j])
    total = jnp.sum(pbuf[...].astype(F32), axis=1).reshape(128, 128)
    change = mm(standardise(total).astype(BF), w_change[...])
    tile_f[...] = mid_all + closing * change
    for i in range(8):
        pair_out[i] = tile_f[pl.ds(i, 16, stride=8), :].astype(BF)
    for half_j in range(2):
        left_device(pbuf.at[half_j], NB - 1, s_p.at[half_j])


def hand_over(*arrays):
    def kernel(*refs):
        for n in range(len(arrays)):
            refs[len(arrays) + n][...] = refs[n][...]

    vmem = pl.BlockSpec(memory_space=pltpu.VMEM)
    return pl.pallas_call(
        kernel,
        out_shape=tuple(jax.ShapeDtypeStruct(a.shape, a.dtype) for a in arrays),
        in_specs=[vmem] * len(arrays),
        out_specs=(vmem,) * len(arrays),
        name="hand_over",
    )(*arrays)


def per_device(
    homolog_tensor,
    couple_tensor,
    probe_matrix,
    lookup_matrix,
    content_matrix,
    scoring_sigmoid_matrix,
    scoring_final_matrix,
    couple_offset_matrix,
    product_first_matrix,
    product_second_matrix,
    product_final_matrix,
    trio_first_matrix,
    trio_second_matrix,
    trio_sigmoid_matrix,
    trio_final_matrix,
):
    operands = (
        homolog_tensor.reshape(256, 256),
        couple_tensor.reshape(128, 128),
        probe_matrix.T,
        lookup_matrix.T,
        content_matrix.T,
        scoring_sigmoid_matrix.T,
        scoring_final_matrix,
        couple_offset_matrix.T,
        product_first_matrix.T,
        product_second_matrix.T,
        product_final_matrix,
        jnp.transpose(trio_first_matrix, (0, 2, 1)),
        jnp.transpose(trio_second_matrix, (0, 2, 1)),
        trio_sigmoid_matrix,
        trio_final_matrix,
    )
    vmem = pl.BlockSpec(memory_space=pltpu.VMEM)
    scratch = [
        ((256, 256), BF),
        ((128, 128), BF),
        ((64, 256), BF),
        ((64, 256), BF),
        ((64, 256), BF),
        ((64, 256), BF),
        ((2, 128), BF),
        ((32, 256), BF),
        ((32, 256), BF),
        ((1024, 128), BF),
        ((128, 128), BF),
        ((128, 128), BF),
        ((32, 256), BF),
        ((8, 32, 256), BF),
        ((32, 128), BF),
        ((8, 32, 128), BF),
        ((16, 16, 256), BF),
        ((16, 128), BF),
        ((8, 16, 128), BF),
        ((16, 128), BF),
        ((16, 16, 128), BF),
        ((4, 4, 32, 128), BF),
        ((4, 64, 256), BF),
        ((4, 32, 128), BF),
        ((128, 128), F32),
        ((32, 128), BF),
        ((8, 32, 128), BF),
        ((32, 128), BF),
        ((2, 8, 32, 128), BF),
        ((8, 32, 128), F32),
        ((2, 8, 32, 128), F32),
        ((2, 64, 128), BF),
        ((2, 4, 64, 128), BF),
        ((128, 128), F32),
        ((16, 8, 128), BF),
        ((4, 16, 8, 128), BF),
        ((2, 128, 64), BF),
        ((2, 128, 64), BF),
        ((2, 128, 128), BF),
        ((2, 128, 128), F32),
    ]
    msa, pairwise = pl.pallas_call(
        kernel,
        out_shape=(
            jax.ShapeDtypeStruct((16, 2, 8, 64), BF),
            jax.ShapeDtypeStruct((8, 16, 128), BF),
        ),
        in_specs=[pl.BlockSpec(memory_space=pltpu.HBM)] * len(operands),
        out_specs=(vmem, vmem),
        scratch_shapes=[pltpu.VMEM(*s) for s in scratch]
        + [pltpu.SemaphoreType.DMA((len(operands),))]
        + [pltpu.SemaphoreType.DMA((2,))] * 11
        + [pltpu.SemaphoreType.DMA((2, 2))],
        compiler_params=pltpu.CompilerParams(
            collective_id=0, has_side_effects=True
        ),
        name="block",
    )(*operands)
    return hand_over(msa.reshape(32, 8, 64), pairwise)


def solution(mesh):
    return jax.shard_map(
        per_device,
        mesh=mesh,
        in_specs=(
            P("col", "row", None),
            P("row", "col", None),
            P(None, "branch"),
            P(None, "branch"),
            P(None, "branch"),
            P(None, "branch"),
            P("branch", None),
            P(None, "branch"),
            P(),
            P(),
            P(),
            P(None, None, "branch"),
            P(None, None, "branch"),
            P(),
            P(),
        ),
        out_specs=(P("col", "row", "branch"), P("row", "col", None)),
        check_vma=False,
    )
```
